256 devices in a mesh: sub: 64 (over x, z_lo, y, core), grp: 4 (over z_hi).
Axes of the slice: x: 4, y: 4, z: 8 (z_hi: 4, z_lo: 2; z = z_hi * 2 + z_lo), core: 2. Of those that a mesh axis runs over, the one named last changes fastest.
Arguments:
- basis: float32 [64, 3, 32, 4, 8, 512], P('sub', None, None, None, None, 'grp'), may hold values from -6 to 6
- material: int32 [64, 4, 8, 512], P('sub', None, None, 'grp'), may hold values from 0 to 7
- kappa_table: float32 [8], replicated, may hold values from 0.1 to 1
Outputs:
- factor: float32 [64, 32, 32], P('sub')
- panel: float32 [64, 8, 32, 32], P('sub')
The draws below stay inside these ranges and needn't reach their ends.
All inputs are finite; a program needn't handle non-finite values.
Results may differ from the reference program's by a relative error of at most 0.0003.
Values sent between devices are 32-bit elements; how exact they have to be, the bound alone decides.
A program may use at most 192 MiB of HBM per device.

```python
import math
import jax
import jax.numpy as jnp
from jax import lax

NV = 32
CX = 4
CY = 8
MATS = 8
YDOMS = 4
SUBDOMAINS = 64
NZ = 512
SUBCELLS = 16384


def set_ends(array, stream_key, least, high):
    index_at = [jax.random.randint(jax.random.fold_in(stream_key, axis), (), 0, length) for axis, length in enumerate(array.shape)]
    main_axis = array.shape.index(max(array.shape))
    next_to = index_at[:main_axis] + [(index_at[main_axis] + 1) % array.shape[main_axis]] + index_at[main_axis + 1:]
    return array.at[tuple(index_at)].set(least).at[tuple(next_to)].set(high)


def level_of(rng, shape, shards, low, high):
    loudness, own = 1.0, jax.random.fold_in(rng, 6)
    for axis_at, parts in shards:
        draws = jnp.exp(jax.random.uniform(jax.random.fold_in(own, axis_at), (parts,), jnp.float32, low / len(shards), high / len(shards)))
        loudness = loudness * jnp.repeat(draws, shape[axis_at] // parts).reshape([-1 if axis == axis_at else 1 for axis in range(len(shape))])
    return loudness


def gaussian(key, shape, deviation, reach, shards=(), kind=jnp.bfloat16):
    drawn = jax.random.normal(key, shape, jnp.float32) * deviation
    if len(shards) > 0:
        drawn = level_of(key, shape, shards, -0.22, 0.18) * drawn
    return jnp.clip(drawn, min=-reach, max=reach).astype(kind)


def setup_inputs(seed: int = 0) -> dict:
    splits = jax.random.split(jax.random.key(seed), 4)
    basis = gaussian(splits[0], (SUBDOMAINS, 3, NV, CX, CY, NZ), 1.0, 6.0, ((0, 64), (5, 4)), jnp.float32)
    material = set_ends(jax.random.randint(splits[1], (SUBDOMAINS, CX, CY, NZ), 0, MATS), jax.random.fold_in(splits[1], 1), 0, MATS - 1).astype(jnp.int32)
    kappa_table = jnp.clip(jnp.exp(jax.random.uniform(splits[2], (MATS,), jnp.float32, math.log(0.1), math.log(1.0))), 0.1, 1.0)
    return dict(basis=basis, material=material, kappa_table=kappa_table)


MIXING = 0.5

def stencil_entries():
    entries = []
    for step_x in (-1, 0, 1):
        for step_y in (-1, 0, 1):
            for step_z in (-1, 0, 1):
                norm_sq = step_x * step_x + step_y * step_y + step_z * step_z
                if norm_sq > 0:
                    entries.append((step_x, step_y, step_z, 0.5 ** (norm_sq - 1), norm_sq))
    return entries

def coupling_blocks(own_basis, padded_kappa, near_basis, extent_x, extent_y, layers):
    center = padded_kappa[1:extent_x + 3, 1:extent_y + 3, 1:layers + 1]
    applied = jnp.zeros((3, own_basis.shape[1], extent_x + 2, extent_y + 2, layers), own_basis.dtype)
    weight_sum = jnp.zeros((extent_x + 2, extent_y + 2, layers), own_basis.dtype)
    for step_x, step_y, step_z, weight, norm_sq in stencil_entries():
        span_x = slice(1 + step_x, extent_x + 3 + step_x)
        span_y = slice(1 + step_y, extent_y + 3 + step_y)
        span_z = slice(1 + step_z, layers + 1 + step_z)
        coupled = weight * 0.5 * (center + padded_kappa[span_x, span_y, span_z])
        shifted = own_basis[:, :, span_x, span_y, span_z]
        projected = step_x * shifted[0] + step_y * shifted[1] + step_z * shifted[2]
        mixed_basis = shifted + MIXING / norm_sq * jnp.stack([step_x * projected, step_y * projected, step_z * projected])
        applied = applied - coupled * mixed_basis
        weight_sum = weight_sum + coupled
    inner_x = slice(1, extent_x + 1)
    inner_y = slice(1, extent_y + 1)
    diagonal = (1.0 + MIXING) * weight_sum[inner_x, inner_y] + 0.5 * center[inner_x, inner_y]
    applied = applied.at[:, :, inner_x, inner_y].add(diagonal * own_basis[:, :, 2:extent_x + 2, 2:extent_y + 2, 1:layers + 1])
    regions_x = [slice(0, 1), slice(1, extent_x + 1), slice(extent_x + 1, extent_x + 2)]
    regions_y = [slice(0, 1), slice(1, extent_y + 1), slice(extent_y + 1, extent_y + 2)]
    blocks = []
    for region_x in regions_x:
        for region_y in regions_y:
            blocks.append(jnp.einsum('kixyz,kjxyz->ij', applied[:, :, region_x, region_y], near_basis[:, :, region_x, region_y], precision=lax.Precision.HIGHEST))
    return jnp.stack(blocks)

def solve_blocks(lower, blocks):
    count = blocks.shape[0]
    width = blocks.shape[1]
    stacked = blocks.transpose(1, 0, 2).reshape(width, count * width)
    solved = jax.scipy.linalg.solve_triangular(lower, stacked, lower=True)
    return solved.reshape(width, count, width).transpose(1, 0, 2)

def reference(basis, material, kappa_table):
    xdoms = SUBDOMAINS // YDOMS
    kappa = jnp.zeros(material.shape, kappa_table.dtype)
    for which in range(MATS):
        kappa = kappa + jnp.where(material == which, kappa_table[which], 0.0)
    grid_kappa = kappa.reshape(xdoms, YDOMS, CX, CY, NZ).transpose(0, 2, 1, 3, 4).reshape(xdoms * CX, YDOMS * CY, NZ)
    grid_basis = basis.reshape(xdoms, YDOMS, 3, NV, CX, CY, NZ).transpose(2, 3, 0, 4, 1, 5, 6).reshape(3, NV, xdoms * CX, YDOMS * CY, NZ)
    kappa_pad = jnp.pad(grid_kappa, ((2, 2), (2, 2), (1, 1)))
    basis_pad = jnp.pad(grid_basis, ((0, 0), (0, 0), (2, 2), (2, 2), (1, 1)))
    zero = jnp.zeros((), jnp.int32)

    def one_subdomain(index):
        start_x = (index // YDOMS * CX).astype(jnp.int32)
        start_y = (index % YDOMS * CY).astype(jnp.int32)
        window_kappa = lax.dynamic_slice(kappa_pad, (start_x, start_y, zero), (CX + 4, CY + 4, NZ + 2))
        window_basis = lax.dynamic_slice(basis_pad, (zero, zero, start_x, start_y, zero), (3, NV, CX + 4, CY + 4, NZ + 2))
        own_basis = jnp.pad(window_basis[:, :, 2:CX + 2, 2:CY + 2, :], ((0, 0), (0, 0), (2, 2), (2, 2), (0, 0)))
        near_basis = window_basis[:, :, 1:CX + 3, 1:CY + 3, 1:NZ + 1]
        blocks = coupling_blocks(own_basis, window_kappa, near_basis, CX, CY, NZ)
        lower = jnp.linalg.cholesky(blocks[4])
        others = jnp.concatenate([blocks[:4], blocks[5:]], axis=0)
        return (lower / jnp.sqrt(3.0 * SUBCELLS), solve_blocks(lower, others))
    factor, panel = lax.map(one_subdomain, jnp.arange(SUBDOMAINS, dtype=jnp.int32))
    return (factor, panel)
```

```python
import functools

import jax
import jax.numpy as jnp
import numpy as np
from jax import lax
from jax.experimental import pallas as pl
from jax.experimental.pallas import tpu as pltpu
from jax.sharding import PartitionSpec as P

YDOMS = 4
XDOMS = 16
SLABS = 4
MESH = pl.DeviceIdType.MESH
F32 = jnp.float32
BF16 = jnp.bfloat16
GHOSTS = 42
ROWS = 144
ALL_NEAR = [(p, r) for p in (-1, 0, 1) for r in (-1, 0, 1) if (p, r) != (0, 0)]
FORWARD = [(0, 1), (1, -1), (1, 0), (1, 1)]


def out_cells():
    cells = [(a, x, y) for a in range(3) for x in range(4) for y in range(8)]
    cells += [(a, 4, y) for a in range(3) for y in range(8)]
    cells += [(a, x, 8) for x in range(4) for a in range(3)]
    cells += [(a, 4, 8) for a in range(3)]
    cells += [(a, 4, -1) for a in range(3)]
    return cells


def stencil_matrix():
    whole = np.zeros((3, ROWS, 96), np.float64)
    for part, step_z in enumerate((0, 1, -1)):
        for row, (a, x, y) in enumerate(out_cells()):
            for p in (-1, 0, 1):
                for r in (-1, 0, 1):
                    o = (p, r, step_z)
                    q = sum(v * v for v in o)
                    if q == 0 or not (0 <= x + p < 4 and 0 <= y + r < 8):
                        continue
                    for b in range(3):
                        g = (1.0 if a == b else 0.0) + 0.5 / q * o[a] * o[b]
                        whole[part, row, b * 32 + (x + p) * 8 + y + r] += 24.0 * 0.5 ** (q - 1) * g
    whole = np.round(whole).reshape(3 * ROWS, 96)
    return np.concatenate([whole, whole], axis=1)


def split(value):
    high = value.astype(BF16)
    low = (value - high.astype(F32)).astype(BF16)
    return jnp.concatenate([high, low], axis=0)


def dot(a, b):
    return lax.dot_general(a, b, (((1,), (0,)), ((), ())), preferred_element_type=F32)


def dot_nt(a, b):
    return lax.dot_general(a, b, (((1,), (1,)), ((), ())), preferred_element_type=F32)


def quadrants(r):
    top = r[:32] + r[32:]
    return top[:, :32] + top[:, 32:]


def kernel(basis, material, table, stencil, factor, panel,
           zs, mat, c_all, fb, rb, ks, packy, gin, gout, khx, khy, khc, ke, kd, kt, k3,
           ss, sgk, qb, nin, fin, bout, bin_,
           lsem, gs, gr, hs, hr, fs, fr, ns, nr, es, er, bs, br):
    s = lax.axis_index("sub")
    g = lax.axis_index("grp")
    i = s // YDOMS
    j = lax.rem(s, YDOMS)

    def near(p, r):
        return lax.rem(i + p + XDOMS, XDOMS) * YDOMS + lax.rem(j + r + YDOMS, YDOMS)

    def inside(p, r):
        ok = jnp.bool_(True)
        if p:
            ok = jnp.logical_and(ok, i < XDOMS - 1 if p > 0 else i > 0)
        if r:
            ok = jnp.logical_and(ok, j < YDOMS - 1 if r > 0 else j > 0)
        return ok

    def slab(d):
        return lax.rem(g + d + SLABS, SLABS)

    def remote(src, dst, send, recv, sub, grp):
        return pltpu.make_async_remote_copy(
            src_ref=src, dst_ref=dst, send_sem=send, recv_sem=recv,
            device_id={"sub": sub, "grp": grp}, device_id_type=MESH)

    load_mat = pltpu.make_async_copy(material, mat, lsem.at[0])
    load_zs = pltpu.make_async_copy(basis, zs, lsem.at[1])
    load_c = pltpu.make_async_copy(stencil, c_all, lsem.at[2])
    load_mat.start()
    load_zs.start()
    load_c.start()
    barrier = pltpu.get_barrier_semaphore()
    for p, r in ALL_NEAR:
        pl.semaphore_signal(barrier, inc=1, device_id={"sub": near(p, r), "grp": g}, device_id_type=MESH)
    for d in (1, 2, 3):
        pl.semaphore_signal(barrier, inc=1, device_id={"sub": s, "grp": slab(d)}, device_id_type=MESH)

    load_mat.wait()
    ids = mat[...]
    kappa = jnp.zeros((32, 128), F32)
    for which in range(8):
        kappa = kappa + jnp.where(ids == which, table[which], 0.0)
    ks[0] = kappa
    for a in range(3):
        k3[32 * a : 32 * a + 32, :] = kappa
    gout[0, 0:32, :] = kappa
    gout[1, 0:32, :] = kappa

    load_zs.wait()
    for a in range(3):
        for y in range(8):
            fb[8 * a + y] = zs[pl.ds(a * 1024 + y, 32, stride=32), :]
    for x in range(4):
        for a in range(3):
            fb[24 + 3 * x + a] = zs[pl.ds(a * 1024 + x * 8, 32, stride=32), :]
    for a in range(3):
        fb[36 + a] = zs[pl.ds(a * 1024 + 7, 32, stride=32), :]

    lane24 = lax.broadcasted_iota(jnp.int32, (24, 128), 1)

    def own(col):
        return jnp.concatenate(
            [zs[pl.ds(pl.multiple_of(a * 1024 + col * 32, 32), 32), :] for a in range(3)], axis=0)

    def edge(col, carry):
        first, last = carry
        u = own(col)
        for k in range(4):
            rows = u[24 * k : 24 * k + 24]
            here = lane24 == 32 * k + col
            first = jnp.where(here, pltpu.roll(rows, 32 * k + col, 1), first)
            last = jnp.where(here, pltpu.roll(rows, lax.rem(32 * k + col + 1, 128), 1), last)
        return first, last

    zero24 = jnp.zeros((24, 128), F32)
    first, last = lax.fori_loop(0, 32, edge, (zero24, zero24))
    gout[0, 32:56, :] = first
    gout[1, 32:56, :] = last

    pl.semaphore_wait(barrier, len(ALL_NEAR) + 3)

    to_low = remote(gout.at[0], gin.at[1], gs.at[0], gr.at[1], s, slab(-1))
    to_high = remote(gout.at[1], gin.at[0], gs.at[1], gr.at[0], s, slab(1))
    to_low.start()
    to_high.start()
    faces = []
    for a in range(3):
        faces.append(remote(fb.at[pl.ds(8 * a, 8)], rb.at[pl.ds(8 * a, 8)], fs.at[a], fr.at[a], near(-1, 0), g))
    faces.append(remote(fb.at[pl.ds(24, 12)], rb.at[pl.ds(24, 12)], fs.at[3], fr.at[3], near(0, -1), g))
    faces.append(remote(fb.at[pl.ds(24, 3)], rb.at[pl.ds(36, 3)], fs.at[4], fr.at[4], near(-1, -1), g))
    faces.append(remote(fb.at[pl.ds(36, 3)], rb.at[pl.ds(39, 3)], fs.at[5], fr.at[5], near(-1, 1), g))
    for copy in faces:
        copy.start()

    to_low.wait_recv()
    to_high.wait_recv()
    lane = lax.broadcasted_iota(jnp.int32, (32, 128), 1)
    low_ok = g > 0
    high_ok = g < SLABS - 1
    k_low = jnp.where(low_ok, gin[0, 0:32, :], 0.0)
    k_high = jnp.where(high_ok, gin[1, 0:32, :], 0.0)
    k_down = jnp.where(lane == 0, pltpu.roll(k_low, 1, 1), pltpu.roll(kappa, 1, 1))
    k_up = jnp.where(lane == 127, pltpu.roll(k_high, 127, 1), pltpu.roll(kappa, 127, 1))
    ks[1] = kappa + 0.5 * (k_down + k_up)
    for e, y in ((0, 0), (1, 7)):
        for which in range(2):
            for x in range(4):
                packy[e, 4 * which + x : 4 * which + x + 1, :] = ks[which, 8 * x + y : 8 * x + y + 1, :]
    halo = [
        remote(ks.at[:, pl.ds(0, 8)], khx.at[1], hs.at[0], hr.at[0], near(-1, 0), g),
        remote(ks.at[:, pl.ds(24, 8)], khx.at[0], hs.at[1], hr.at[1], near(1, 0), g),
        remote(packy.at[0], khy.at[1], hs.at[2], hr.at[2], near(0, -1), g),
        remote(packy.at[1], khy.at[0], hs.at[3], hr.at[3], near(0, 1), g),
        remote(packy.at[0], khc.at[3], hs.at[4], hr.at[4], near(-1, -1), g),
        remote(packy.at[1], khc.at[0], hs.at[5], hr.at[5], near(1, 1), g),
        remote(packy.at[1], khc.at[2], hs.at[6], hr.at[6], near(-1, 1), g),
        remote(packy.at[0], khc.at[1], hs.at[7], hr.at[7], near(1, -1), g),
    ]
    for copy in halo:
        copy.start()

    load_c.wait()
    lane96 = lax.broadcasted_iota(jnp.int32, (96, 128), 1)

    def spread(packed):
        return jnp.concatenate(
            [packed if k == 0 else pltpu.roll(packed, 128 - 32 * k, 1) for k in range(4)], axis=0)

    h_high = spread(jnp.where(high_ok, gin[1, 32:56, :], 0.0))
    h_low = spread(jnp.where(low_ok, gin[0, 32:56, :], 0.0))
    kc_high = jnp.concatenate([k_high[:, 0:1]] * 3, axis=0)
    kc_low = jnp.concatenate([k_low[:, 127:128]] * 3, axis=0)
    edges = jnp.where(lane96 < 32, h_high, pltpu.roll(h_low, 32, 1))
    kedges = jnp.where(lane96 < 32, h_high * kc_high, pltpu.roll(h_low * kc_low, 32, 1))
    edges = jnp.where(lane96 < 64, edges, pltpu.roll(kedges, 64, 1))
    ch = dot(c_all[...], split(edges))
    ch_high = ch[ROWS : 2 * ROWS]
    ch_low = ch[2 * ROWS : 3 * ROWS]
    lane_all = lax.broadcasted_iota(jnp.int32, (ROWS, 128), 1)
    lane48 = lax.broadcasted_iota(jnp.int32, (48, 128), 1)
    kpair = jnp.concatenate([k3[...], k3[...]], axis=1)
    c_ghost = jnp.concatenate([c_all[part * ROWS + 96 : (part + 1) * ROWS, :] for part in range(3)], axis=0)

    def pair(step, carry):
        u = jnp.concatenate([own(2 * step), own(2 * step + 1)], axis=1)
        r = dot(c_all[...], split(u))
        rk = dot(c_ghost, split(u * kpair))
        for half in range(2):
            col = 2 * step + half
            part = r[:, 128 * half : 128 * half + 128]
            up = jnp.where(lane_all == 127, pltpu.roll(ch_high, 127 - col, 1), pltpu.roll(part[ROWS : 2 * ROWS], 127, 1))
            down = jnp.where(lane_all == 0, pltpu.roll(ch_low, 96 - col, 1), pltpu.roll(part[2 * ROWS :], 1, 1))
            ss[pl.ds(pl.multiple_of(col * ROWS, ROWS), ROWS), :] = part[:ROWS] + up + down
            part = rk[:, 128 * half : 128 * half + 128]
            up = jnp.where(lane48 == 127, pltpu.roll(ch_high[96:], 63 - col, 1), pltpu.roll(part[48:96], 127, 1))
            down = jnp.where(lane48 == 0, pltpu.roll(ch_low[96:], 32 - col, 1), pltpu.roll(part[96:], 1, 1))
            sgk[pl.ds(pl.multiple_of(col * 48, 48), 48), :] = part[:48] + up + down
        return carry

    lax.fori_loop(0, 16, pair, 0)

    for copy in halo:
        copy.wait_recv()
    ke[...] = jnp.zeros_like(ke)
    for x in range(4):
        ke[1 + x, 1:9, :] = ks[1, 8 * x : 8 * x + 8, :]
        ke[1 + x, 0:1, :] = jnp.where(inside(0, -1), khy[0, 4 + x : 5 + x, :], 0.0)
        ke[1 + x, 9:10, :] = jnp.where(inside(0, 1), khy[1, 4 + x : 5 + x, :], 0.0)
    ke[0, 1:9, :] = jnp.where(inside(-1, 0), khx[0, 1], 0.0)
    ke[5, 1:9, :] = jnp.where(inside(1, 0), khx[1, 1], 0.0)
    ke[0, 0:1, :] = jnp.where(inside(-1, -1), khc[0, 7:8, :], 0.0)
    ke[0, 9:10, :] = jnp.where(inside(-1, 1), khc[1, 7:8, :], 0.0)
    ke[5, 0:1, :] = jnp.where(inside(1, -1), khc[2, 4:5, :], 0.0)
    ke[5, 9:10, :] = jnp.where(inside(1, 1), khc[3, 4:5, :], 0.0)
    planes = [ke[x, 1:9, :] + 0.5 * (ke[x, 0:8, :] + ke[x, 2:10, :]) for x in range(6)]
    for x in range(4):
        smooth = planes[x + 1] + 0.5 * (planes[x] + planes[x + 2])
        kd[8 * x : 8 * x + 8, :] = 228.0 * ks[0, 8 * x : 8 * x + 8, :] + 36.0 * smooth
    for a in range(3):
        kt[8 * a : 8 * a + 8, :] = khx[1, 0]
        for x in range(4):
            kt[24 + 3 * x + a : 25 + 3 * x + a, :] = khy[1, x : x + 1, :]
        kt[36 + a : 37 + a, :] = khc[3, 0:1, :]
        kt[39 + a : 40 + a, :] = khc[2, 0:1, :]
    kt[42:48, :] = jnp.zeros((6, 128), F32)

    def inner(step, total):
        start_z = (step // 4) * 1024 + lax.rem(step, 4) * 8
        start_s = step * 8
        start_k = lax.rem(step, 4) * 8
        left, right = [], []
        for y in range(8):
            z = zs[pl.ds(start_z + y, 32, stride=32), :]
            v = ss[pl.ds(start_s + y, 32, stride=ROWS), :]
            left.append(z)
            right.append(kd[pl.ds(start_k + y, 1), :] * z - ks[0, pl.ds(start_k + y, 1), :] * v)
        left = split(jnp.concatenate(left, axis=1))
        right = split(jnp.concatenate(right, axis=1))
        return total + dot_nt(left, right)

    total = quadrants(lax.fori_loop(0, 12, inner, jnp.zeros((64, 64), F32)))
    total = (total + total.T) * (1.0 / 48.0)
    nin[g, :, 0:32] = total
    sums = [remote(nin.at[g], nin.at[g], ns.at[d - 1], nr.at[d - 1], s, slab(d)) for d in (1, 2, 3)]
    for copy in sums:
        copy.start()

    def ghost(step, carry):
        tiles = []
        for y in range(8):
            m = step * 8 + y
            tiles.append(kt[pl.ds(m, 1), :] * ss[pl.ds(96 + m, 32, stride=ROWS), :] + sgk[pl.ds(m, 32, stride=48), :])
        qb[:, pl.ds(pl.multiple_of(step * 1024, 1024), 1024)] = split(jnp.concatenate(tiles, axis=1))
        return carry

    lax.fori_loop(0, 6, ghost, 0)

    def coupled(start, count):
        f = split(jnp.concatenate([rb[start + t] for t in range(count)], axis=1))
        return dot_nt(qb[:, start * 128 : (start + count) * 128], f)

    lane32 = lax.broadcasted_iota(jnp.int32, (32, 128), 1)
    lane8 = lax.broadcasted_iota(jnp.int32, (8, 128), 1)

    def place(parts):
        result = jnp.zeros((32, 128), F32)
        for at, block in parts.items():
            wide = jnp.concatenate([block, jnp.zeros((32, 96), F32)], axis=1)
            wide = wide if at == 0 else pltpu.roll(wide, 32 * at, 1)
            result = jnp.where(lane32 // 32 == at, wide, result)
        return result

    def turned(block):
        wide = jnp.concatenate([block.T, jnp.zeros((32, 96), F32)], axis=1)
        result = wide[0:8]
        for k in range(1, 4):
            result = jnp.where(lane8 // 32 == k, pltpu.roll(wide[8 * k : 8 * k + 8], 32 * k, 1), result)
        return result

    sent = []

    def give(which, at, blocks):
        tile = place(blocks)
        fin[which, g] = tile
        for d in (1, 2, 3):
            copy = remote(fin.at[which, g], fin.at[which, g], es.at[which, d - 1], er.at[which, d - 1], s, slab(d))
            copy.start()
            sent.append(copy)
        for b, block in blocks.items():
            bout[b] = turned(block)
            for d in range(4):
                copy = remote(bout.at[b], bin_.at[b, g], bs.at[b, d], br.at[b, d], near(*FORWARD[b]), slab(d))
                copy.start()
                sent.append(copy)

    def finished(b, value):
        return jnp.where(inside(*FORWARD[b]), quadrants(value) * (-1.0 / 48.0), 0.0)

    for which in (3, 4, 5):
        faces[which].wait_recv()
    give(0, 0, {0: finished(0, coupled(24, 12)), 1: finished(1, coupled(39, 3)), 3: finished(3, coupled(36, 3))})
    value = jnp.zeros((64, 64), F32)
    for a in range(3):
        faces[a].wait_recv()
        value = value + coupled(8 * a, 8)
    give(1, 2, {2: finished(2, value)})

    for copy in sums:
        copy.wait_recv()
    row32 = lax.broadcasted_iota(jnp.int32, (32, 128), 0)
    m = nin[0] + nin[1] + nin[2] + nin[3]
    m = jnp.where(lane32 < 32, m, jnp.where(lane32 == row32 + 32, 1.0, 0.0))
    lower = jnp.zeros((32, 128), F32)
    for k in range(32):
        pivot = m[k : k + 1, k : k + 1]
        r = lax.rsqrt(pivot)
        r = r * (1.5 - 0.5 * pivot * r * r)
        col = m[:, k : k + 1] * r
        line = m[k : k + 1, :] * r
        lower = jnp.where(jnp.logical_and(lane32 == k, row32 >= k), col, lower)
        m = jnp.where(row32 > k, m - col * line, jnp.where(row32 == k, line, m))
    factor[...] = lower[:, 0:32] * (1.0 / np.sqrt(49152.0))
    inverse = m[:, 32:64]

    for copy in sent:
        copy.wait_recv()
    ahead = jnp.zeros((32, 128), F32)
    for h in range(SLABS):
        ahead = ahead + (fin[0, h] + fin[1, h])
    behind = [jnp.zeros((8, 128), F32)] * 4
    packed = [bin_[b, 0] + bin_[b, 1] + bin_[b, 2] + bin_[b, 3] for b in range(4)]
    order = [3, 2, 1, 0]
    rows = []
    for k in range(4):
        result = jnp.zeros((8, 128), F32)
        for at in range(4):
            shift = (32 * (at - k)) % 128
            moved = packed[order[at]] if shift == 0 else pltpu.roll(packed[order[at]], shift, 1)
            result = jnp.where(lane8 // 32 == at, moved, result)
        rows.append(result)
    every = jnp.concatenate([jnp.concatenate(rows, axis=0), ahead], axis=1)
    panel[...] = lax.dot_general(inverse, every, (((1,), (0,)), ((), ())), precision=lax.Precision.HIGHEST,
                                 preferred_element_type=F32)

    to_low.wait_send()
    to_high.wait_send()
    for copy in faces + halo + sums + sent:
        copy.wait_send()


def shards(stencil, basis, material, kappa_table):
    any_space = pl.BlockSpec(memory_space=pl.ANY)
    vmem = pl.BlockSpec(memory_space=pltpu.VMEM)
    dma = pltpu.SemaphoreType.DMA
    factor, panel = pl.pallas_call(
        kernel,
        out_shape=(jax.ShapeDtypeStruct((32, 32), F32), jax.ShapeDtypeStruct((32, 256), F32)),
        in_specs=[any_space, any_space, pl.BlockSpec(memory_space=pltpu.SMEM), any_space],
        out_specs=(vmem, vmem),
        scratch_shapes=[
            pltpu.VMEM((3072, 128), F32),
            pltpu.VMEM((32, 128), jnp.int32),
            pltpu.VMEM((3 * ROWS, 192), BF16),
            pltpu.VMEM((39, 32, 128), F32),
            pltpu.VMEM((42, 32, 128), F32),
            pltpu.VMEM((2, 32, 128), F32),
            pltpu.VMEM((2, 8, 128), F32),
            pltpu.VMEM((2, 56, 128), F32),
            pltpu.VMEM((2, 56, 128), F32),
            pltpu.VMEM((2, 2, 8, 128), F32),
            pltpu.VMEM((2, 8, 128), F32),
            pltpu.VMEM((4, 8, 128), F32),
            pltpu.VMEM((6, 16, 128), F32),
            pltpu.VMEM((32, 128), F32),
            pltpu.VMEM((48, 128), F32),
            pltpu.VMEM((96, 128), F32),
            pltpu.VMEM((32 * ROWS, 128), F32),
            pltpu.VMEM((32 * 48, 128), F32),
            pltpu.VMEM((64, 6 * 1024), BF16),
            pltpu.VMEM((4, 32, 128), F32),
            pltpu.VMEM((2, 4, 32, 128), F32),
            pltpu.VMEM((4, 8, 128), F32),
            pltpu.VMEM((4, 4, 8, 128), F32),
            dma((3,)), dma((2,)), dma((2,)), dma((8,)), dma((8,)), dma((6,)), dma((6,)),
            dma((3,)), dma((3,)), dma((2, 3)), dma((2, 3)), dma((4, 4)), dma((4, 4)),
        ],
        compiler_params=pltpu.CompilerParams(
            collective_id=0, has_side_effects=True, vmem_limit_bytes=40 * 2**20),
        name="coarse_blocks",
    )(basis.reshape(3072, 128), material.reshape(32, 128), kappa_table, stencil)
    panel = panel.reshape(32, 8, 32).transpose(1, 0, 2)
    return factor[None], panel[None]


def solution(mesh):
    placed = (P(), P("sub", None, None, None, None, "grp"), P("sub", None, None, "grp"), P())
    call = jax.shard_map(
        shards,
        mesh=mesh,
        in_specs=placed,
        out_specs=(P("sub", None, None), P("sub", None, None, None)),
        check_vma=False,
    )
    matrix = stencil_matrix()

    def run(basis, material, kappa_table):
        return call(jnp.asarray(matrix, BF16), basis, material, kappa_table)

    return run
```

```python
import functools

import jax
import jax.numpy as jnp
import numpy as np
from jax import lax
from jax.experimental import pallas as pl
from jax.experimental.pallas import tpu as pltpu
from jax.sharding import PartitionSpec as P

YDOMS = 4
XDOMS = 16
SLABS = 4
MESH = pl.DeviceIdType.MESH
F32 = jnp.float32
BF16 = jnp.bfloat16
GHOSTS = 42
ROWS = 144
ALL_NEAR = [(p, r) for p in (-1, 0, 1) for r in (-1, 0, 1) if (p, r) != (0, 0)]
FORWARD = [(0, 1), (1, -1), (1, 0), (1, 1)]


def out_cells():
    cells = [(a, x, y) for a in range(3) for x in range(4) for y in range(8)]
    cells += [(a, 4, y) for a in range(3) for y in range(8)]
    cells += [(a, x, 8) for x in range(4) for a in range(3)]
    cells += [(a, 4, 8) for a in range(3)]
    cells += [(a, 4, -1) for a in range(3)]
    return cells


def stencil_matrix():
    whole = np.zeros((3, ROWS, 96), np.float64)
    for part, step_z in enumerate((0, 1, -1)):
        for row, (a, x, y) in enumerate(out_cells()):
            for p in (-1, 0, 1):
                for r in (-1, 0, 1):
                    o = (p, r, step_z)
                    q = sum(v * v for v in o)
                    if q == 0 or not (0 <= x + p < 4 and 0 <= y + r < 8):
                        continue
                    for b in range(3):
                        g = (1.0 if a == b else 0.0) + 0.5 / q * o[a] * o[b]
                        whole[part, row, b * 32 + (x + p) * 8 + y + r] += 24.0 * 0.5 ** (q - 1) * g
    whole = np.round(whole).reshape(3 * ROWS, 96)
    return np.concatenate([whole, whole], axis=1)


def split(value):
    high = value.astype(BF16)
    low = (value - high.astype(F32)).astype(BF16)
    return jnp.concatenate([high, low], axis=0)


def dot(a, b):
    return lax.dot_general(a, b, (((1,), (0,)), ((), ())), preferred_element_type=F32)


def dot_nt(a, b):
    return lax.dot_general(a, b, (((1,), (1,)), ((), ())), preferred_element_type=F32)


def dot_tn(a, b):
    return lax.dot_general(a, b, (((0,), (0,)), ((), ())), precision=lax.Precision.HIGHEST, preferred_element_type=F32)


def quadrants(r):
    top = r[:32] + r[32:]
    return top[:, :32] + top[:, 32:]


def kernel(basis, material, table, stencil, factor, panel,
           zs, mat, c_all, fb, rb, ks, packy, gin, gout, khx, khy, khc, ke, kd, kt, k3,
           ss, sgk, qb, nin, fin, bout, bin_, tab, c_in,
           lsem, gs, gr, hs, hr, fs, fr, ns, nr, es, er, bs, br):
    s = lax.axis_index("sub")
    g = lax.axis_index("grp")
    i = s // YDOMS
    j = lax.rem(s, YDOMS)

    def near(p, r):
        return lax.rem(i + p + XDOMS, XDOMS) * YDOMS + lax.rem(j + r + YDOMS, YDOMS)

    def inside(p, r):
        ok = jnp.bool_(True)
        if p:
            ok = jnp.logical_and(ok, i < XDOMS - 1 if p > 0 else i > 0)
        if r:
            ok = jnp.logical_and(ok, j < YDOMS - 1 if r > 0 else j > 0)
        return ok

    def slab(d):
        return lax.rem(g + d + SLABS, SLABS)

    def remote(src, dst, send, recv, sub, grp):
        return pltpu.make_async_remote_copy(
            src_ref=src, dst_ref=dst, send_sem=send, recv_sem=recv,
            device_id={"sub": sub, "grp": grp}, device_id_type=MESH)

    barrier = pltpu.get_barrier_semaphore()
    for p, r in ALL_NEAR:
        pl.semaphore_signal(barrier, inc=1, device_id={"sub": near(p, r), "grp": g}, device_id_type=MESH)
    for d in (1, 2, 3):
        pl.semaphore_signal(barrier, inc=1, device_id={"sub": s, "grp": slab(d)}, device_id_type=MESH)

    load_mat = pltpu.make_async_copy(material, mat, lsem.at[0])
    load_zs = pltpu.make_async_copy(basis, zs, lsem.at[1])
    load_c = pltpu.make_async_copy(stencil, c_in, lsem.at[2])
    load_tab = pltpu.make_async_copy(table, tab, lsem.at[3])
    load_mat.start()
    load_tab.start()
    load_zs.start()
    load_c.start()

    load_mat.wait()
    load_tab.wait()
    ids = mat[...]
    kappa = jnp.zeros((32, 128), F32)
    for which in range(8):
        kappa = kappa + jnp.where(ids == which, tab[which], 0.0)
    ks[...] = kappa
    for e, y in ((0, 0), (1, 7)):
        for x in range(4):
            packy[e, x : x + 1, :] = ks[8 * x + y : 8 * x + y + 1, :]
    for a in range(3):
        k3[32 * a : 32 * a + 32, :] = kappa
    gout[0, 0:32, :] = kappa
    gout[1, 0:32, :] = kappa

    load_zs.wait()
    for a in range(3):
        for y in range(8):
            fb[8 * a + y] = zs[pl.ds(a * 1024 + y, 32, stride=32), :]
    for x in range(4):
        for a in range(3):
            fb[24 + 3 * x + a] = zs[pl.ds(a * 1024 + x * 8, 32, stride=32), :]
    for a in range(3):
        fb[36 + a] = zs[pl.ds(a * 1024 + 7, 32, stride=32), :]

    lane24 = lax.broadcasted_iota(jnp.int32, (24, 128), 1)

    def own(col):
        return jnp.concatenate(
            [zs[pl.ds(pl.multiple_of(a * 1024 + col * 32, 32), 32), :] for a in range(3)], axis=0)

    def edge(col, carry):
        first, last = carry
        u = own(col)
        for k in range(4):
            rows = u[24 * k : 24 * k + 24]
            here = lane24 == 32 * k + col
            first = jnp.where(here, pltpu.roll(rows, 32 * k + col, 1), first)
            last = jnp.where(here, pltpu.roll(rows, lax.rem(32 * k + col + 1, 128), 1), last)
        return first, last

    zero24 = jnp.zeros((24, 128), F32)
    first, last = lax.fori_loop(0, 32, edge, (zero24, zero24))
    gout[0, 32:56, :] = first
    gout[1, 32:56, :] = last

    load_c.wait()
    c_all[...] = c_in[...].astype(BF16)
    pl.semaphore_wait(barrier, len(ALL_NEAR) + 3)

    to_low = remote(gout.at[0], gin.at[1], gs.at[0], gr.at[1], s, slab(-1))
    to_high = remote(gout.at[1], gin.at[0], gs.at[1], gr.at[0], s, slab(1))
    to_low.start()
    to_high.start()
    halo = [
        remote(ks.at[pl.ds(0, 8)], khx.at[1], hs.at[0], hr.at[0], near(-1, 0), g),
        remote(ks.at[pl.ds(24, 8)], khx.at[0], hs.at[1], hr.at[1], near(1, 0), g),
        remote(packy.at[0], khy.at[1], hs.at[2], hr.at[2], near(0, -1), g),
        remote(packy.at[1], khy.at[0], hs.at[3], hr.at[3], near(0, 1), g),
        remote(packy.at[0], khc.at[3], hs.at[4], hr.at[4], near(-1, -1), g),
        remote(packy.at[1], khc.at[0], hs.at[5], hr.at[5], near(1, 1), g),
        remote(packy.at[1], khc.at[2], hs.at[6], hr.at[6], near(-1, 1), g),
        remote(packy.at[0], khc.at[1], hs.at[7], hr.at[7], near(1, -1), g),
    ]
    for copy in halo:
        copy.start()
    faces = []
    for a in range(3):
        faces.append(remote(fb.at[pl.ds(8 * a, 8)], rb.at[pl.ds(8 * a, 8)], fs.at[a], fr.at[a], near(-1, 0), g))
    faces.append(remote(fb.at[pl.ds(24, 12)], rb.at[pl.ds(24, 12)], fs.at[3], fr.at[3], near(0, -1), g))
    faces.append(remote(fb.at[pl.ds(24, 3)], rb.at[pl.ds(36, 3)], fs.at[4], fr.at[4], near(-1, -1), g))
    faces.append(remote(fb.at[pl.ds(36, 3)], rb.at[pl.ds(39, 3)], fs.at[5], fr.at[5], near(-1, 1), g))
    for copy in faces:
        copy.start()

    to_low.wait_recv()
    to_high.wait_recv()
    lane = lax.broadcasted_iota(jnp.int32, (32, 128), 1)
    low_ok = g > 0
    high_ok = g < SLABS - 1
    k_low = jnp.where(low_ok, gin[0, 0:32, :], 0.0)
    k_high = jnp.where(high_ok, gin[1, 0:32, :], 0.0)
    lane96 = lax.broadcasted_iota(jnp.int32, (96, 128), 1)

    def spread(packed):
        return jnp.concatenate(
            [packed if k == 0 else pltpu.roll(packed, 128 - 32 * k, 1) for k in range(4)], axis=0)

    h_high = spread(jnp.where(high_ok, gin[1, 32:56, :], 0.0))
    h_low = spread(jnp.where(low_ok, gin[0, 32:56, :], 0.0))
    kc_high = jnp.concatenate([k_high[:, 0:1]] * 3, axis=0)
    kc_low = jnp.concatenate([k_low[:, 127:128]] * 3, axis=0)
    edges = jnp.where(lane96 < 32, h_high, pltpu.roll(h_low, 32, 1))
    kedges = jnp.where(lane96 < 32, h_high * kc_high, pltpu.roll(h_low * kc_low, 32, 1))
    edges = jnp.where(lane96 < 64, edges, pltpu.roll(kedges, 64, 1))
    ch = dot(c_all[...], split(edges))
    ch_high = ch[ROWS : 2 * ROWS]
    ch_low = ch[2 * ROWS : 3 * ROWS]
    lane_all = lax.broadcasted_iota(jnp.int32, (ROWS, 128), 1)
    lane48 = lax.broadcasted_iota(jnp.int32, (48, 128), 1)
    kpair = jnp.concatenate([k3[...], k3[...]], axis=1)
    c_ghost = jnp.concatenate([c_all[part * ROWS + 96 : (part + 1) * ROWS, :] for part in range(3)], axis=0)

    def pair(step, carry):
        u = jnp.concatenate([own(2 * step), own(2 * step + 1)], axis=1)
        r = dot(c_all[...], split(u))
        rk = dot(c_ghost, split(u * kpair))
        for half in range(2):
            col = 2 * step + half
            part = r[:, 128 * half : 128 * half + 128]
            up = jnp.where(lane_all == 127, pltpu.roll(ch_high, 127 - col, 1), pltpu.roll(part[ROWS : 2 * ROWS], 127, 1))
            down = jnp.where(lane_all == 0, pltpu.roll(ch_low, 96 - col, 1), pltpu.roll(part[2 * ROWS :], 1, 1))
            ss[pl.ds(pl.multiple_of(col * ROWS, ROWS), ROWS), :] = part[:ROWS] + up + down
            part = rk[:, 128 * half : 128 * half + 128]
            up = jnp.where(lane48 == 127, pltpu.roll(ch_high[96:], 63 - col, 1), pltpu.roll(part[48:96], 127, 1))
            down = jnp.where(lane48 == 0, pltpu.roll(ch_low[96:], 32 - col, 1), pltpu.roll(part[96:], 1, 1))
            sgk[pl.ds(pl.multiple_of(col * 48, 48), 48), :] = part[:48] + up + down
        return carry

    lax.fori_loop(0, 16, pair, 0)

    for copy in halo:
        copy.wait_recv()
    ke[...] = jnp.zeros_like(ke)
    for x in range(4):
        ke[1 + x, 1:9, :] = ks[8 * x : 8 * x + 8, :]
        ke[1 + x, 0:1, :] = jnp.where(inside(0, -1), khy[0, x : 1 + x, :], 0.0)
        ke[1 + x, 9:10, :] = jnp.where(inside(0, 1), khy[1, x : 1 + x, :], 0.0)
    ke[0, 1:9, :] = jnp.where(inside(-1, 0), khx[0], 0.0)
    ke[5, 1:9, :] = jnp.where(inside(1, 0), khx[1], 0.0)
    ke[0, 0:1, :] = jnp.where(inside(-1, -1), khc[0, 3:4, :], 0.0)
    ke[0, 9:10, :] = jnp.where(inside(-1, 1), khc[1, 3:4, :], 0.0)
    ke[5, 0:1, :] = jnp.where(inside(1, -1), khc[2, 0:1, :], 0.0)
    ke[5, 9:10, :] = jnp.where(inside(1, 1), khc[3, 0:1, :], 0.0)
    planes = [ke[x, 1:9, :] + 0.5 * (ke[x, 0:8, :] + ke[x, 2:10, :]) for x in range(6)]
    smooth = jnp.concatenate([planes[x + 1] + 0.5 * (planes[x] + planes[x + 2]) for x in range(4)], axis=0)
    up = jnp.where(lane == 127, 0.0, pltpu.roll(smooth, 127, 1))
    down = jnp.where(lane == 0, 0.0, pltpu.roll(smooth, 1, 1))
    kd[...] = 228.0 * ks[...] + 36.0 * smooth + 18.0 * (up + down)
    for a in range(3):
        kt[8 * a : 8 * a + 8, :] = khx[1]
        for x in range(4):
            kt[24 + 3 * x + a : 25 + 3 * x + a, :] = khy[1, x : x + 1, :]
        kt[36 + a : 37 + a, :] = khc[3, 0:1, :]
        kt[39 + a : 40 + a, :] = khc[2, 0:1, :]
    kt[42:48, :] = jnp.zeros((6, 128), F32)

    near_low = jnp.concatenate([smooth[:, 0:1]] * 3, axis=0) * 18.0
    near_high = jnp.concatenate([smooth[:, 127:128]] * 3, axis=0) * 18.0
    layers = jnp.concatenate([h_low, h_high], axis=0)
    weighted = jnp.concatenate([h_low * near_low, h_high * near_high], axis=0)
    outside = dot_tn(weighted, layers)[:32, :32]

    def ghost(step, carry):
        tiles = []
        for y in range(8):
            m = step * 8 + y
            tiles.append(kt[pl.ds(m, 1), :] * ss[pl.ds(96 + m, 32, stride=ROWS), :] + sgk[pl.ds(m, 32, stride=48), :])
        qb[:, pl.ds(pl.multiple_of(step * 1024, 1024), 1024)] = split(jnp.concatenate(tiles, axis=1))
        return carry

    lax.fori_loop(0, 6, ghost, 0)

    def inner(step, total):
        start_z = (step // 4) * 1024 + lax.rem(step, 4) * 8
        start_s = step * 8
        start_k = lax.rem(step, 4) * 8
        left, right = [], []
        for y in range(8):
            z = zs[pl.ds(start_z + y, 32, stride=32), :]
            v = ss[pl.ds(start_s + y, 32, stride=ROWS), :]
            left.append(z)
            right.append(kd[pl.ds(start_k + y, 1), :] * z - ks[pl.ds(start_k + y, 1), :] * v)
        left = split(jnp.concatenate(left, axis=1))
        right = split(jnp.concatenate(right, axis=1))
        return total + dot_nt(left, right)

    total = quadrants(lax.fori_loop(0, 12, inner, jnp.zeros((64, 64), F32))) + outside
    total = (total + total.T) * (1.0 / 48.0)
    nin[g, :, 0:32] = total
    sums = [remote(nin.at[g], nin.at[g], ns.at[d - 1], nr.at[d - 1], s, slab(d)) for d in (1, 2, 3)]
    for copy in sums:
        copy.start()

    def coupled(start, count):
        f = split(jnp.concatenate([rb[start + t] for t in range(count)], axis=1))
        return dot_nt(qb[:, start * 128 : (start + count) * 128], f)

    lane32 = lax.broadcasted_iota(jnp.int32, (32, 128), 1)
    lane8 = lax.broadcasted_iota(jnp.int32, (8, 128), 1)

    def place(parts):
        result = jnp.zeros((32, 128), F32)
        for at, block in parts.items():
            wide = jnp.concatenate([block, jnp.zeros((32, 96), F32)], axis=1)
            wide = wide if at == 0 else pltpu.roll(wide, 32 * at, 1)
            result = jnp.where(lane32 // 32 == at, wide, result)
        return result

    def turned(block):
        wide = jnp.concatenate([block.T, jnp.zeros((32, 96), F32)], axis=1)
        result = wide[0:8]
        for k in range(1, 4):
            result = jnp.where(lane8 // 32 == k, pltpu.roll(wide[8 * k : 8 * k + 8], 32 * k, 1), result)
        return result

    sent = []

    def give(which, at, blocks):
        tile = place(blocks)
        fin[which, g] = tile
        for d in (1, 2, 3):
            copy = remote(fin.at[which, g], fin.at[which, g], es.at[which, d - 1], er.at[which, d - 1], s, slab(d))
            copy.start()
            sent.append(copy)
        for b, block in blocks.items():
            bout[b] = turned(block)
            for d in range(4):
                copy = remote(bout.at[b], bin_.at[b, g], bs.at[b, d], br.at[b, d], near(*FORWARD[b]), slab(d))
                copy.start()
                sent.append(copy)

    def finished(b, value):
        return jnp.where(inside(*FORWARD[b]), quadrants(value) * (-1.0 / 48.0), 0.0)

    for which in (3, 4, 5):
        faces[which].wait_recv()
    give(0, 0, {0: finished(0, coupled(24, 12)), 1: finished(1, coupled(39, 3)), 3: finished(3, coupled(36, 3))})
    value = jnp.zeros((64, 64), F32)
    for a in range(3):
        faces[a].wait_recv()
        value = value + coupled(8 * a, 8)
    give(1, 2, {2: finished(2, value)})

    for copy in sums:
        copy.wait_recv()
    row32 = lax.broadcasted_iota(jnp.int32, (32, 128), 0)
    m = nin[0] + nin[1] + nin[2] + nin[3]
    m = jnp.where(lane32 < 32, m, jnp.where(lane32 == row32 + 32, 1.0, 0.0))
    lower = jnp.zeros((32, 128), F32)
    for k in range(32):
        pivot = m[k : k + 1, k : k + 1]
        r = lax.rsqrt(pivot)
        r = r * (1.5 - 0.5 * pivot * r * r)
        col = m[:, k : k + 1] * r
        line = m[k : k + 1, :] * r
        lower = jnp.where(jnp.logical_and(lane32 == k, row32 >= k), col, lower)
        m = jnp.where(row32 > k, m - col * line, jnp.where(row32 == k, line, m))
    factor[...] = lower[:, 0:32] * (1.0 / np.sqrt(49152.0))
    inverse = m[:, 32:64]

    for copy in sent:
        copy.wait_recv()
    ahead = jnp.zeros((32, 128), F32)
    for h in range(SLABS):
        ahead = ahead + (fin[0, h] + fin[1, h])
    behind = [jnp.zeros((8, 128), F32)] * 4
    packed = [bin_[b, 0] + bin_[b, 1] + bin_[b, 2] + bin_[b, 3] for b in range(4)]
    order = [3, 2, 1, 0]
    rows = []
    for k in range(4):
        result = jnp.zeros((8, 128), F32)
        for at in range(4):
            shift = (32 * (at - k)) % 128
            moved = packed[order[at]] if shift == 0 else pltpu.roll(packed[order[at]], shift, 1)
            result = jnp.where(lane8 // 32 == at, moved, result)
        rows.append(result)
    every = jnp.concatenate([jnp.concatenate(rows, axis=0), ahead], axis=1)
    panel[...] = lax.dot_general(inverse, every, (((1,), (0,)), ((), ())), precision=lax.Precision.HIGHEST,
                                 preferred_element_type=F32)

    to_low.wait_send()
    to_high.wait_send()
    for copy in faces + halo + sums + sent:
        copy.wait_send()


def shards(stencil, basis, material, kappa_table):
    hbm = pl.BlockSpec(memory_space=pltpu.HBM)
    vmem = pl.BlockSpec(memory_space=pltpu.VMEM)
    dma = pltpu.SemaphoreType.DMA
    operands = (basis.reshape(3072, 128), material.reshape(32, 128), kappa_table, stencil)
    factor, panel = pl.pallas_call(
        kernel,
        out_shape=(jax.ShapeDtypeStruct((32, 32), F32), jax.ShapeDtypeStruct((32, 256), F32)),
        in_specs=[hbm, hbm, hbm, hbm],
        out_specs=(vmem, vmem),
        scratch_shapes=[
            pltpu.VMEM((3072, 128), F32),
            pltpu.VMEM((32, 128), jnp.int32),
            pltpu.VMEM((3 * ROWS, 192), BF16),
            pltpu.VMEM((39, 32, 128), F32),
            pltpu.VMEM((42, 32, 128), F32),
            pltpu.VMEM((32, 128), F32),
            pltpu.VMEM((2, 8, 128), F32),
            pltpu.VMEM((2, 56, 128), F32),
            pltpu.VMEM((2, 56, 128), F32),
            pltpu.VMEM((2, 8, 128), F32),
            pltpu.VMEM((2, 8, 128), F32),
            pltpu.VMEM((4, 8, 128), F32),
            pltpu.VMEM((6, 16, 128), F32),
            pltpu.VMEM((32, 128), F32),
            pltpu.VMEM((48, 128), F32),
            pltpu.VMEM((96, 128), F32),
            pltpu.VMEM((32 * ROWS, 128), F32),
            pltpu.VMEM((32 * 48, 128), F32),
            pltpu.VMEM((64, 6 * 1024), BF16),
            pltpu.VMEM((4, 32, 128), F32),
            pltpu.VMEM((2, 4, 32, 128), F32),
            pltpu.VMEM((4, 8, 128), F32),
            pltpu.VMEM((4, 4, 8, 128), F32),
            pltpu.SMEM((8,), F32),
            pltpu.VMEM((3 * ROWS, 192), F32),
            dma((4,)), dma((2,)), dma((2,)), dma((8,)), dma((8,)), dma((6,)), dma((6,)),
            dma((3,)), dma((3,)), dma((2, 3)), dma((2, 3)), dma((4, 4)), dma((4, 4)),
        ],
        compiler_params=pltpu.CompilerParams(
            collective_id=0, has_side_effects=True, vmem_limit_bytes=40 * 2**20),
        name="coarse_blocks",
    )(*(pltpu.with_memory_space_constraint(value, pltpu.HBM) for value in operands))
    panel = panel.reshape(32, 8, 32).transpose(1, 0, 2)
    return factor[None], panel[None]


def solution(mesh):
    placed = (P(), P("sub", None, None, None, None, "grp"), P("sub", None, None, "grp"), P())
    call = jax.shard_map(
        shards,
        mesh=mesh,
        in_specs=placed,
        out_specs=(P("sub", None, None), P("sub", None, None, None)),
        check_vma=False,
    )
    matrix = stencil_matrix()

    def run(basis, material, kappa_table):
        return call(jnp.asarray(matrix, F32), basis, material, kappa_table)

    return run
```

```python
import functools

import jax
import jax.numpy as jnp
import numpy as np
from jax import lax
from jax.experimental import pallas as pl
from jax.experimental.pallas import tpu as pltpu
from jax.sharding import PartitionSpec as P

YDOMS = 4
XDOMS = 16
SLABS = 4
MESH = pl.DeviceIdType.MESH
F32 = jnp.float32
BF16 = jnp.bfloat16
GHOSTS = 42
ROWS = 144
ALL_NEAR = [(p, r) for p in (-1, 0, 1) for r in (-1, 0, 1) if (p, r) != (0, 0)]
UNROLL_E = 4
UNROLL_S = 2
UNROLL_N = 2


def out_cells():
    cells = [(a, x, y) for a in range(3) for x in range(4) for y in range(8)]
    cells += [(a, 4, y) for a in range(3) for y in range(8)]
    cells += [(a, x, 8) for x in range(4) for a in range(3)]
    cells += [(a, 4, 8) for a in range(3)]
    cells += [(a, 4, -1) for a in range(3)]
    return cells


def stencil_matrix():
    whole = np.zeros((3, ROWS, 96), np.float64)
    for part, step_z in enumerate((0, 1, -1)):
        for row, (a, x, y) in enumerate(out_cells()):
            for p in (-1, 0, 1):
                for r in (-1, 0, 1):
                    o = (p, r, step_z)
                    q = sum(v * v for v in o)
                    if q == 0 or not (0 <= x + p < 4 and 0 <= y + r < 8):
                        continue
                    for b in range(3):
                        g = (1.0 if a == b else 0.0) + 0.5 / q * o[a] * o[b]
                        whole[part, row, b * 32 + (x + p) * 8 + y + r] += 24.0 * 0.5 ** (q - 1) * g
    whole = np.round(whole).reshape(3 * ROWS, 96)
    return np.concatenate([whole, whole], axis=1)


def split(value):
    high = value.astype(BF16)
    low = (value - high.astype(F32)).astype(BF16)
    return jnp.concatenate([high, low], axis=0)


def dot(a, b):
    return lax.dot_general(a, b, (((1,), (0,)), ((), ())), preferred_element_type=F32)


def dot_nt(a, b):
    return lax.dot_general(a, b, (((1,), (1,)), ((), ())), preferred_element_type=F32)


def dot_tn(a, b):
    return lax.dot_general(a, b, (((0,), (0,)), ((), ())), precision=lax.Precision.HIGHEST, preferred_element_type=F32)


def quadrants(r):
    top = r[:32] + r[32:]
    return top[:, :32] + top[:, 32:]


def kernel(basis, material, table, stencil, factor, panel,
           zs, mat, c_all, fb, rb, ks, packy, gin, gout, khx, khy, khc, ke, kd, kt, k3,
           ss, sgk, qb, qg, qc, nin, inbox, outbox, tab, c_in,
           lsem, gs, gr, hs, hr, fs, fr, cs, cr, ns, nr, bs, br):
    s = lax.axis_index("sub")
    g = lax.axis_index("grp")
    i = s // YDOMS
    j = lax.rem(s, YDOMS)

    def near(p, r):
        return lax.rem(i + p + XDOMS, XDOMS) * YDOMS + lax.rem(j + r + YDOMS, YDOMS)

    def inside(p, r):
        ok = jnp.bool_(True)
        if p:
            ok = jnp.logical_and(ok, i < XDOMS - 1 if p > 0 else i > 0)
        if r:
            ok = jnp.logical_and(ok, j < YDOMS - 1 if r > 0 else j > 0)
        return ok

    def slab(d):
        return lax.rem(g + d + SLABS, SLABS)

    def remote(src, dst, send, recv, sub, grp):
        return pltpu.make_async_remote_copy(
            src_ref=src, dst_ref=dst, send_sem=send, recv_sem=recv,
            device_id={"sub": sub, "grp": grp}, device_id_type=MESH)

    barrier = pltpu.get_barrier_semaphore()
    for p, r in ALL_NEAR:
        pl.semaphore_signal(barrier, inc=1, device_id={"sub": near(p, r), "grp": g}, device_id_type=MESH)
    for d in (1, 2, 3):
        pl.semaphore_signal(barrier, inc=1, device_id={"sub": s, "grp": slab(d)}, device_id_type=MESH)

    load_mat = pltpu.make_async_copy(material, mat, lsem.at[0])
    load_zs = pltpu.make_async_copy(basis, zs, lsem.at[1])
    load_c = pltpu.make_async_copy(stencil, c_in, lsem.at[2])
    load_tab = pltpu.make_async_copy(table, tab, lsem.at[3])
    load_mat.start()
    load_tab.start()
    load_zs.start()
    load_c.start()

    load_mat.wait()
    load_tab.wait()
    ids = mat[...]
    kappa = jnp.zeros((32, 128), F32)
    for which in range(8):
        kappa = kappa + jnp.where(ids == which, tab[which], 0.0)
    ks[...] = kappa
    for e, y in ((0, 0), (1, 7)):
        for x in range(4):
            packy[e, x : x + 1, :] = ks[8 * x + y : 8 * x + y + 1, :]
    for a in range(3):
        k3[32 * a : 32 * a + 32, :] = kappa
    gout[0, 0:32, :] = kappa
    gout[1, 0:32, :] = kappa

    load_zs.wait()
    for a in range(3):
        for y in range(8):
            fb[8 * a + y] = zs[pl.ds(a * 1024 + y, 32, stride=32), :]
    for x in range(4):
        for a in range(3):
            fb[24 + 3 * x + a] = zs[pl.ds(a * 1024 + x * 8, 32, stride=32), :]
    lane24 = lax.broadcasted_iota(jnp.int32, (24, 128), 1)

    def own(col):
        return jnp.concatenate(
            [zs[pl.ds(pl.multiple_of(a * 1024 + col * 32, 32), 32), :] for a in range(3)], axis=0)

    def edge(col, carry):
        first, last = carry
        u = own(col)
        for k in range(4):
            rows = u[24 * k : 24 * k + 24]
            here = lane24 == 32 * k + col
            first = jnp.where(here, pltpu.roll(rows, 32 * k + col, 1), first)
            last = jnp.where(here, pltpu.roll(rows, lax.rem(32 * k + col + 1, 128), 1), last)
        return first, last

    zero24 = jnp.zeros((24, 128), F32)
    first, last = lax.fori_loop(0, 32, edge, (zero24, zero24), unroll=UNROLL_E)
    gout[0, 32:56, :] = first
    gout[1, 32:56, :] = last

    load_c.wait()
    c_all[...] = c_in[...].astype(BF16)
    pl.semaphore_wait(barrier, len(ALL_NEAR) + 3)

    to_low = remote(gout.at[0], gin.at[1], gs.at[0], gr.at[1], s, slab(-1))
    to_high = remote(gout.at[1], gin.at[0], gs.at[1], gr.at[0], s, slab(1))
    to_low.start()
    to_high.start()
    halo = [
        remote(ks.at[pl.ds(0, 8)], khx.at[1], hs.at[0], hr.at[0], near(-1, 0), g),
        remote(ks.at[pl.ds(24, 8)], khx.at[0], hs.at[1], hr.at[1], near(1, 0), g),
        remote(packy.at[0], khy.at[1], hs.at[2], hr.at[2], near(0, -1), g),
        remote(packy.at[1], khy.at[0], hs.at[3], hr.at[3], near(0, 1), g),
        remote(packy.at[0], khc.at[3], hs.at[4], hr.at[4], near(-1, -1), g),
        remote(packy.at[1], khc.at[0], hs.at[5], hr.at[5], near(1, 1), g),
        remote(packy.at[1], khc.at[2], hs.at[6], hr.at[6], near(-1, 1), g),
        remote(packy.at[0], khc.at[1], hs.at[7], hr.at[7], near(1, -1), g),
    ]
    for copy in halo:
        copy.start()
    faces = [
        (1, 0, remote(fb.at[pl.ds(8 * a, 8)], rb.at[pl.ds(8 * a, 8)], fs.at[a], fr.at[a], near(-1, 0), g))
        for a in range(3)
    ]
    faces.append((0, 1, remote(fb.at[pl.ds(24, 12)], rb.at[pl.ds(24, 12)], fs.at[3], fr.at[3], near(0, -1), g)))
    for p, r, copy in faces:
        pl.when(inside(-p, -r))(copy.start)

    kpair = jnp.concatenate([k3[...], k3[...]], axis=1)
    c_ghost = jnp.concatenate([c_all[part * ROWS + 96 : (part + 1) * ROWS, :] for part in range(3)], axis=0)
    lane_all = lax.broadcasted_iota(jnp.int32, (ROWS, 128), 1)
    lane48 = lax.broadcasted_iota(jnp.int32, (48, 128), 1)

    def pair(step, carry):
        u = jnp.concatenate([own(2 * step), own(2 * step + 1)], axis=1)
        r = dot(c_all[...], split(u))
        rk = dot(c_ghost, split(u * kpair))
        for half in range(2):
            col = 2 * step + half
            part = r[:, 128 * half : 128 * half + 128]
            up = jnp.where(lane_all == 127, 0.0, pltpu.roll(part[ROWS : 2 * ROWS], 127, 1))
            down = jnp.where(lane_all == 0, 0.0, pltpu.roll(part[2 * ROWS :], 1, 1))
            ss[pl.ds(pl.multiple_of(col * ROWS, ROWS), ROWS), :] = part[:ROWS] + up + down
            part = rk[:, 128 * half : 128 * half + 128]
            up = jnp.where(lane48 == 127, 0.0, pltpu.roll(part[48:96], 127, 1))
            down = jnp.where(lane48 == 0, 0.0, pltpu.roll(part[96:], 1, 1))
            sgk[pl.ds(pl.multiple_of(col * 48, 48), 48), :] = part[:48] + up + down
        return carry

    lax.fori_loop(0, 16, pair, 0, unroll=UNROLL_S)

    to_low.wait_recv()
    to_high.wait_recv()
    lane = lax.broadcasted_iota(jnp.int32, (32, 128), 1)
    low_ok = g > 0
    high_ok = g < SLABS - 1
    k_low = jnp.where(low_ok, gin[0, 0:32, :], 0.0)
    k_high = jnp.where(high_ok, gin[1, 0:32, :], 0.0)
    lane96 = lax.broadcasted_iota(jnp.int32, (96, 128), 1)

    def spread(packed):
        return jnp.concatenate(
            [packed if k == 0 else pltpu.roll(packed, 128 - 32 * k, 1) for k in range(4)], axis=0)

    h_high = spread(jnp.where(high_ok, gin[1, 32:56, :], 0.0))
    h_low = spread(jnp.where(low_ok, gin[0, 32:56, :], 0.0))
    kc_high = jnp.concatenate([k_high[:, 0:1]] * 3, axis=0)
    kc_low = jnp.concatenate([k_low[:, 127:128]] * 3, axis=0)
    edges = jnp.where(lane96 < 32, h_high, pltpu.roll(h_low, 32, 1))
    kedges = jnp.where(lane96 < 32, h_high * kc_high, pltpu.roll(h_low * kc_low, 32, 1))
    edges = jnp.where(lane96 < 64, edges, pltpu.roll(kedges, 64, 1))
    ch = dot(c_all[...], split(edges))

    for copy in halo:
        copy.wait_recv()
    ke[...] = jnp.zeros_like(ke)
    for x in range(4):
        ke[1 + x, 1:9, :] = ks[8 * x : 8 * x + 8, :]
        ke[1 + x, 0:1, :] = jnp.where(inside(0, -1), khy[0, x : 1 + x, :], 0.0)
        ke[1 + x, 9:10, :] = jnp.where(inside(0, 1), khy[1, x : 1 + x, :], 0.0)
    ke[0, 1:9, :] = jnp.where(inside(-1, 0), khx[0], 0.0)
    ke[5, 1:9, :] = jnp.where(inside(1, 0), khx[1], 0.0)
    ke[0, 0:1, :] = jnp.where(inside(-1, -1), khc[0, 3:4, :], 0.0)
    ke[0, 9:10, :] = jnp.where(inside(-1, 1), khc[1, 3:4, :], 0.0)
    ke[5, 0:1, :] = jnp.where(inside(1, -1), khc[2, 0:1, :], 0.0)
    ke[5, 9:10, :] = jnp.where(inside(1, 1), khc[3, 0:1, :], 0.0)
    planes = [ke[x, 1:9, :] + 0.5 * (ke[x, 0:8, :] + ke[x, 2:10, :]) for x in range(6)]
    smooth = jnp.concatenate([planes[x + 1] + 0.5 * (planes[x] + planes[x + 2]) for x in range(4)], axis=0)
    up = jnp.where(lane == 127, 0.0, pltpu.roll(smooth, 127, 1))
    down = jnp.where(lane == 0, 0.0, pltpu.roll(smooth, 1, 1))
    kd[...] = 228.0 * ks[...] + 36.0 * smooth + 18.0 * (up + down)
    for a in range(3):
        kt[8 * a : 8 * a + 8, :] = khx[1]
        for x in range(4):
            kt[24 + 3 * x + a : 25 + 3 * x + a, :] = khy[1, x : x + 1, :]
        kt[36 + a : 37 + a, :] = khc[3, 0:1, :]
        kt[39 + a : 40 + a, :] = khc[2, 0:1, :]
    kt[42:48, :] = jnp.zeros((6, 128), F32)

    def column(tile, at):
        return jnp.concatenate([tile[:, at : at + 1]] * 3, axis=0)

    own_low = spread(gout[0, 32:56, :])
    own_high = spread(gout[1, 32:56, :])
    left = jnp.concatenate([
        h_low * (18.0 * column(smooth, 0)), h_high * (18.0 * column(smooth, 127)),
        -own_high * column(kappa, 127), -own_low * column(kappa, 0)], axis=0)
    right = jnp.concatenate([
        h_low, h_high, ch[ROWS : ROWS + 96], pltpu.roll(ch[2 * ROWS : 2 * ROWS + 96], 96, 1)], axis=0)
    outside = dot_tn(left, right)[:32, :32]

    g_high = ch[ROWS + 96 : 2 * ROWS]
    g_low = ch[2 * ROWS + 96 :]
    g_high = kt[:, 127:128] * g_high + pltpu.roll(g_high, 64, 1)
    g_low = kt[:, 0:1] * g_low + pltpu.roll(g_low, 64, 1)
    turn = jnp.where(lane48 < 32, g_high, g_low).T
    turn_high = jnp.concatenate([turn[0:32], jnp.zeros((32, 80), F32)], axis=1)
    turn_low = jnp.concatenate([turn[32:64], jnp.zeros((32, 80), F32)], axis=1)

    def ghost(step, carry):
        tiles = []
        for y in range(8):
            m = step * 8 + y
            tile = kt[pl.ds(m, 1), :] * ss[pl.ds(96 + m, 32, stride=ROWS), :] + sgk[pl.ds(m, 32, stride=48), :]
            high = jnp.where(lane == 127, pltpu.roll(turn_high, 127 - m, 1), 0.0)
            tile = tile + jnp.where(lane == 0, pltpu.roll(turn_low, lax.rem(128 - m, 128), 1), high)
            qg[m] = tile
            tiles.append(tile)
        qb[:, pl.ds(pl.multiple_of(step * 1024, 1024), 1024)] = split(jnp.concatenate(tiles, axis=1))
        return carry

    lax.fori_loop(0, 6, ghost, 0)
    corners = [
        (0, 1, remote(qg.at[pl.ds(36, 3)], qc.at[0], cs.at[0], cr.at[0], near(0, 1), g)),
        (0, -1, remote(qg.at[pl.ds(39, 3)], qc.at[1], cs.at[1], cr.at[1], near(0, -1), g)),
    ]
    for p, r, copy in corners:
        pl.when(inside(p, r))(copy.start)

    def inner(step, total):
        start_z = (step // 4) * 1024 + lax.rem(step, 4) * 8
        start_s = step * 8
        start_k = lax.rem(step, 4) * 8
        left, right = [], []
        for y in range(8):
            z = zs[pl.ds(start_z + y, 32, stride=32), :]
            v = ss[pl.ds(start_s + y, 32, stride=ROWS), :]
            left.append(z)
            right.append(kd[pl.ds(start_k + y, 1), :] * z - ks[pl.ds(start_k + y, 1), :] * v)
        left = split(jnp.concatenate(left, axis=1))
        right = split(jnp.concatenate(right, axis=1))
        return total + dot_nt(left, right)

    total = quadrants(lax.fori_loop(0, 12, inner, jnp.zeros((64, 64), F32), unroll=UNROLL_N)) + outside
    total = (total + total.T) * (1.0 / 48.0)
    nin[g, :, 0:32] = total
    sums = [remote(nin.at[g], nin.at[g], ns.at[d - 1], nr.at[d - 1], s, slab(d)) for d in (1, 2, 3)]
    for copy in sums:
        copy.start()

    def face(start, count):
        return split(jnp.concatenate([rb[start + t] for t in range(count)], axis=1))

    lane32 = lax.broadcasted_iota(jnp.int32, (32, 128), 1)
    lane8 = lax.broadcasted_iota(jnp.int32, (8, 128), 1)

    def pack(block):
        wide = jnp.concatenate([block, jnp.zeros((32, 96), F32)], axis=1)
        result = wide[0:8]
        for k in range(1, 4):
            result = jnp.where(lane8 // 32 == k, pltpu.roll(wide[8 * k : 8 * k + 8], 32 * k, 1), result)
        return result

    def scaled(value, ok):
        return jnp.where(ok, quadrants(value) * (-1.0 / 48.0), 0.0)

    sent = []

    def give(src, slot, count, sub, which, slabs):
        for d in slabs:
            copy = remote(src, inbox.at[g, pl.ds(slot, count)], bs.at[which, d], br.at[which, d], sub, slab(d))
            copy.start()
            sent.append(copy)

    pl.when(inside(0, 1))(faces[3][2].wait_recv)
    block = scaled(dot_nt(qb[:, 24 * 128 : 36 * 128], face(24, 12)), inside(0, 1))
    inbox[g, 4] = pack(block)
    outbox[0] = pack(block.T)
    give(inbox.at[g, pl.ds(4, 1)], 4, 1, s, 0, (1, 2, 3))
    give(outbox.at[pl.ds(0, 1)], 3, 1, near(0, 1), 1, range(4))

    for p, r, copy in corners:
        pl.when(inside(-p, -r))(copy.wait_recv)
    side = [split(jnp.concatenate([qc[e, a] for a in range(3)], axis=1)) for e in range(2)]
    value = jnp.zeros((64, 64), F32)
    value_low = jnp.zeros((64, 64), F32)
    value_high = jnp.zeros((64, 64), F32)
    for a in range(3):
        pl.when(inside(1, 0))(faces[a][2].wait_recv)
        f = face(8 * a, 8)
        value = value + dot_nt(qb[:, a * 1024 : (a + 1) * 1024], f)
        value_low = value_low + dot_nt(side[0][:, 128 * a : 128 * a + 128], f[:, 0:128])
        value_high = value_high + dot_nt(side[1][:, 128 * a : 128 * a + 128], f[:, 896:1024])
    block = scaled(value, inside(1, 0))
    block_low = scaled(value_low, inside(1, -1))
    block_high = scaled(value_high, inside(1, 1))
    outbox[1] = pack(block_low.T)
    outbox[2] = pack(block.T)
    outbox[3] = pack(block_high.T)
    give(outbox.at[pl.ds(1, 3)], 0, 3, near(1, 0), 2, range(4))
    outbox[4] = pack(block_low)
    give(outbox.at[pl.ds(4, 1)], 7, 1, near(0, -1), 3, range(4))
    outbox[5] = pack(block_high)
    give(outbox.at[pl.ds(5, 1)], 5, 1, near(0, 1), 4, range(4))
    inbox[g, 6] = pack(block)
    give(inbox.at[g, pl.ds(6, 1)], 6, 1, s, 5, (1, 2, 3))

    for copy in sums:
        copy.wait_recv()
    row32 = lax.broadcasted_iota(jnp.int32, (32, 128), 0)
    m = nin[0] + nin[1] + nin[2] + nin[3]
    m = jnp.where(lane32 < 32, m, jnp.where(lane32 == row32 + 32, 1.0, 0.0))
    lower = jnp.zeros((32, 128), F32)
    for k in range(32):
        pivot = m[k : k + 1, k : k + 1]
        r = lax.rsqrt(pivot)
        r = r * (1.5 - 0.5 * pivot * r * r)
        col = m[:, k : k + 1] * r
        line = m[k : k + 1, :] * r
        lower = jnp.where(jnp.logical_and(lane32 == k, row32 >= k), col, lower)
        m = jnp.where(row32 > k, m - col * line, jnp.where(row32 == k, line, m))
    factor[...] = lower[:, 0:32] * (1.0 / np.sqrt(49152.0))
    inverse = m[:, 32:64]

    for copy in sent:
        copy.wait_recv()
    packed = [inbox[0, b] + inbox[1, b] + inbox[2, b] + inbox[3, b] for b in range(8)]
    halves = []
    for part in range(2):
        rows = []
        for k in range(4):
            result = jnp.zeros((8, 128), F32)
            for at in range(4):
                shift = (32 * (at - k)) % 128
                moved = packed[4 * part + at]
                moved = moved if shift == 0 else pltpu.roll(moved, shift, 1)
                result = jnp.where(lane8 // 32 == at, moved, result)
            rows.append(result)
        halves.append(jnp.concatenate(rows, axis=0))
    every = jnp.concatenate(halves, axis=1)
    panel[...] = lax.dot_general(inverse, every, (((1,), (0,)), ((), ())), precision=lax.Precision.HIGHEST,
                                 preferred_element_type=F32)

    to_low.wait_send()
    to_high.wait_send()
    for copy in halo + sums + sent:
        copy.wait_send()
    for p, r, copy in faces:
        pl.when(inside(-p, -r))(copy.wait_send)
    for p, r, copy in corners:
        pl.when(inside(p, r))(copy.wait_send)


def shards(stencil, basis, material, kappa_table):
    hbm = pl.BlockSpec(memory_space=pltpu.HBM)
    vmem = pl.BlockSpec(memory_space=pltpu.VMEM)
    dma = pltpu.SemaphoreType.DMA
    operands = (basis.reshape(3072, 128), material.reshape(32, 128), kappa_table, stencil)
    factor, panel = pl.pallas_call(
        kernel,
        out_shape=(jax.ShapeDtypeStruct((32, 32), F32), jax.ShapeDtypeStruct((32, 256), F32)),
        in_specs=[hbm, hbm, hbm, hbm],
        out_specs=(vmem, vmem),
        scratch_shapes=[
            pltpu.VMEM((3072, 128), F32),
            pltpu.VMEM((32, 128), jnp.int32),
            pltpu.VMEM((3 * ROWS, 192), BF16),
            pltpu.VMEM((36, 32, 128), F32),
            pltpu.VMEM((36, 32, 128), F32),
            pltpu.VMEM((32, 128), F32),
            pltpu.VMEM((2, 8, 128), F32),
            pltpu.VMEM((2, 56, 128), F32),
            pltpu.VMEM((2, 56, 128), F32),
            pltpu.VMEM((2, 8, 128), F32),
            pltpu.VMEM((2, 8, 128), F32),
            pltpu.VMEM((4, 8, 128), F32),
            pltpu.VMEM((6, 16, 128), F32),
            pltpu.VMEM((32, 128), F32),
            pltpu.VMEM((48, 128), F32),
            pltpu.VMEM((96, 128), F32),
            pltpu.VMEM((32 * ROWS, 128), F32),
            pltpu.VMEM((32 * 48, 128), F32),
            pltpu.VMEM((64, 6 * 1024), BF16),
            pltpu.VMEM((48, 32, 128), F32),
            pltpu.VMEM((2, 3, 32, 128), F32),
            pltpu.VMEM((4, 32, 128), F32),
            pltpu.VMEM((4, 8, 8, 128), F32),
            pltpu.VMEM((6, 8, 128), F32),
            pltpu.SMEM((8,), F32),
            pltpu.VMEM((3 * ROWS, 192), F32),
            dma((4,)), dma((2,)), dma((2,)), dma((8,)), dma((8,)), dma((4,)), dma((4,)), dma((2,)), dma((2,)),
            dma((3,)), dma((3,)), dma((6, 4)), dma((6, 4)),
        ],
        compiler_params=pltpu.CompilerParams(
            collective_id=0, has_side_effects=True, vmem_limit_bytes=40 * 2**20),
        name="coarse_blocks",
    )(*(pltpu.with_memory_space_constraint(value, pltpu.HBM) for value in operands))
    panel = panel.reshape(32, 8, 32).transpose(1, 0, 2)
    return factor[None], panel[None]


def solution(mesh):
    placed = (P(), P("sub", None, None, None, None, "grp"), P("sub", None, None, "grp"), P())
    call = jax.shard_map(
        shards,
        mesh=mesh,
        in_specs=placed,
        out_specs=(P("sub", None, None), P("sub", None, None, None)),
        check_vma=False,
    )
    matrix = stencil_matrix()

    def run(basis, material, kappa_table):
        return call(jnp.asarray(matrix, F32), basis, material, kappa_table)

    return run
```

```python
import functools

import jax
import jax.numpy as jnp
import numpy as np
from jax import lax
from jax.experimental import pallas as pl
from jax.experimental.pallas import tpu as pltpu
from jax.sharding import PartitionSpec as P

YDOMS = 4
XDOMS = 16
SLABS = 4
MESH = pl.DeviceIdType.MESH
F32 = jnp.float32
BF16 = jnp.bfloat16
GHOSTS = 42
ROWS = 144
ALL_NEAR = [(p, r) for p in (-1, 0, 1) for r in (-1, 0, 1) if (p, r) != (0, 0)]
UNROLL_E = 8
UNROLL_S = 2
UNROLL_N = 2


def out_cells():
    cells = [(a, x, y) for a in range(3) for x in range(4) for y in range(8)]
    cells += [(a, 4, y) for a in range(3) for y in range(8)]
    cells += [(a, x, 8) for x in range(4) for a in range(3)]
    cells += [(a, 4, 8) for a in range(3)]
    cells += [(a, 4, -1) for a in range(3)]
    return cells


def stencil_matrix():
    whole = np.zeros((3, ROWS, 96), np.float64)
    for part, step_z in enumerate((0, 1, -1)):
        for row, (a, x, y) in enumerate(out_cells()):
            for p in (-1, 0, 1):
                for r in (-1, 0, 1):
                    o = (p, r, step_z)
                    q = sum(v * v for v in o)
                    if q == 0 or not (0 <= x + p < 4 and 0 <= y + r < 8):
                        continue
                    for b in range(3):
                        g = (1.0 if a == b else 0.0) + 0.5 / q * o[a] * o[b]
                        whole[part, row, b * 32 + (x + p) * 8 + y + r] += 24.0 * 0.5 ** (q - 1) * g
    whole = np.round(whole).reshape(3 * ROWS, 96)
    return np.concatenate([whole, whole], axis=1)


def split(value):
    high = value.astype(BF16)
    low = (value - high.astype(F32)).astype(BF16)
    return jnp.concatenate([high, low], axis=0)


def dot(a, b):
    return lax.dot_general(a, b, (((1,), (0,)), ((), ())), preferred_element_type=F32)


def dot_nt(a, b):
    return lax.dot_general(a, b, (((1,), (1,)), ((), ())), preferred_element_type=F32)


def dot_tn(a, b):
    return lax.dot_general(a, b, (((0,), (0,)), ((), ())), precision=lax.Precision.HIGHEST, preferred_element_type=F32)


def quadrants(r):
    top = r[:32] + r[32:]
    return top[:, :32] + top[:, 32:]


def kernel(basis, planes, material, table, stencil, factor, panel,
           zs, mat, c_all, fb, rx, ry, ks, packy, gin, gout, khx, khy, khc, ke, kd, kt, k3,
           ss, sgk, qb, qg, qc, nin, inbox, outbox, tab, c_in,
           hello, ready, lsem, gs, gr, hs, hr, fs, fr, cs, cr, ns, nr, bs, br):
    s = lax.axis_index("sub")
    g = lax.axis_index("grp")
    i = s // YDOMS
    j = lax.rem(s, YDOMS)

    def near(p, r):
        return lax.rem(i + p + XDOMS, XDOMS) * YDOMS + lax.rem(j + r + YDOMS, YDOMS)

    def inside(p, r):
        ok = i >= 0
        if p:
            ok = jnp.logical_and(ok, i < XDOMS - 1 if p > 0 else i > 0)
        if r:
            ok = jnp.logical_and(ok, j < YDOMS - 1 if r > 0 else j > 0)
        return ok

    def slab(d):
        return lax.rem(g + d + SLABS, SLABS)

    def remote(src, dst, send, recv, sub, grp):
        return pltpu.make_async_remote_copy(
            src_ref=src, dst_ref=dst, send_sem=send, recv_sem=recv,
            device_id={"sub": sub, "grp": grp}, device_id_type=MESH)

    barrier = pltpu.get_barrier_semaphore()
    entered = g
    for p, r in ALL_NEAR:
        entered = entered + inside(p, r).astype(jnp.int32)

        @pl.when(inside(p, r))
        def _():
            pl.semaphore_signal(barrier, inc=1, device_id={"sub": near(p, r), "grp": g}, device_id_type=MESH)

    for d in (1, 2, 3):

        @pl.when(g + d < SLABS)
        def _():
            pl.semaphore_signal(barrier, inc=1, device_id={"sub": s, "grp": slab(d)}, device_id_type=MESH)

    load_mat = pltpu.make_async_copy(material, mat, lsem.at[0])
    load_zs = pltpu.make_async_copy(basis, zs, lsem.at[1])
    load_c = pltpu.make_async_copy(stencil, c_in, lsem.at[2])
    load_tab = pltpu.make_async_copy(table, tab, lsem.at[3])
    load_mat.start()
    load_tab.start()
    load_zs.start()
    load_c.start()

    load_mat.wait()
    load_tab.wait()
    ids = mat[...]
    kappa = jnp.zeros((32, 128), F32)
    for which in range(8):
        kappa = kappa + jnp.where(ids == which, tab[which], 0.0)
    ks[...] = kappa
    for e, y in ((0, 0), (1, 7)):
        for x in range(4):
            packy[e, x : x + 1, :] = ks[8 * x + y : 8 * x + y + 1, :]
    for a in range(3):
        k3[32 * a : 32 * a + 32, :] = kappa
    gout[0, 0:32, :] = kappa
    gout[1, 0:32, :] = kappa

    load_zs.wait()
    for x in range(4):
        for a in range(3):
            fb[3 * x + a] = zs[pl.ds(a * 1024 + x * 8, 32, stride=32), :]
    pl.semaphore_wait(barrier, entered)
    for d in (1, 2, 3):

        @pl.when(g >= d)
        def _():
            pl.semaphore_signal(hello.at[min(d, 2) - 1], inc=1, device_id={"sub": s, "grp": slab(-d)}, device_id_type=MESH)

    halo = [
        (-1, 0, remote(ks.at[pl.ds(0, 8)], khx.at[1], hs.at[0], hr.at[0], near(-1, 0), g)),
        (1, 0, remote(ks.at[pl.ds(24, 8)], khx.at[0], hs.at[1], hr.at[1], near(1, 0), g)),
        (0, -1, remote(packy.at[0], khy.at[1], hs.at[2], hr.at[2], near(0, -1), g)),
        (0, 1, remote(packy.at[1], khy.at[0], hs.at[3], hr.at[3], near(0, 1), g)),
        (-1, -1, remote(packy.at[0], khc.at[3], hs.at[4], hr.at[4], near(-1, -1), g)),
        (1, 1, remote(packy.at[1], khc.at[0], hs.at[5], hr.at[5], near(1, 1), g)),
        (-1, 1, remote(packy.at[1], khc.at[2], hs.at[6], hr.at[6], near(-1, 1), g)),
        (1, -1, remote(packy.at[0], khc.at[1], hs.at[7], hr.at[7], near(1, -1), g)),
    ]
    for p, r, copy in halo:
        pl.when(inside(p, r))(copy.start)
    faces = [
        (1, 0, remote(planes.at[pl.ds(32 * a, 32), pl.ds(0, 8)], rx.at[pl.ds(32 * a, 32)], fs.at[a], fr.at[a], near(-1, 0), g))
        for a in range(3)
    ]
    faces.append((0, 1, remote(fb, ry, fs.at[3], fr.at[3], near(0, -1), g)))
    for p, r, copy in faces[:1]:
        pl.when(inside(-p, -r))(copy.start)
    lane24 = lax.broadcasted_iota(jnp.int32, (24, 128), 1)

    def own(col):
        return jnp.concatenate(
            [zs[pl.ds(pl.multiple_of(a * 1024 + col * 32, 32), 32), :] for a in range(3)], axis=0)

    def edge(col, carry):
        first, last = carry
        u = own(col)
        for k in range(4):
            rows = u[24 * k : 24 * k + 24]
            here = lane24 == 32 * k + col
            first = jnp.where(here, pltpu.roll(rows, 32 * k + col, 1), first)
            last = jnp.where(here, pltpu.roll(rows, lax.rem(32 * k + col + 1, 128), 1), last)
        return first, last

    zero24 = jnp.zeros((24, 128), F32)
    first, last = lax.fori_loop(0, 32, edge, (zero24, zero24), unroll=UNROLL_E)
    gout[0, 32:56, :] = first
    gout[1, 32:56, :] = last

    to_low = remote(gout.at[0], gin.at[1], gs.at[0], gr.at[1], s, slab(-1))
    to_high = remote(gout.at[1], gin.at[0], gs.at[1], gr.at[0], s, slab(1))
    low_ok = g > 0
    high_ok = g < SLABS - 1
    pl.when(low_ok)(to_low.start)

    @pl.when(high_ok)
    def _():
        pl.semaphore_wait(hello.at[0], 1)
        to_high.start()

    for p, r, copy in faces[1:]:
        pl.when(inside(-p, -r))(copy.start)
    load_c.wait()
    c_all[...] = c_in[...].astype(BF16)
    kpair = jnp.concatenate([k3[...], k3[...]], axis=1)
    c_ghost = jnp.concatenate([c_all[part * ROWS + 96 : (part + 1) * ROWS, :] for part in range(3)], axis=0)
    lane_all = lax.broadcasted_iota(jnp.int32, (ROWS, 128), 1)
    lane48 = lax.broadcasted_iota(jnp.int32, (48, 128), 1)

    def pair(step, carry):
        u = jnp.concatenate([own(2 * step), own(2 * step + 1)], axis=1)
        r = dot(c_all[...], split(u))
        rk = dot(c_ghost, split(u * kpair))
        for half in range(2):
            col = 2 * step + half
            part = r[:, 128 * half : 128 * half + 128]
            up = jnp.where(lane_all == 127, 0.0, pltpu.roll(part[ROWS : 2 * ROWS], 127, 1))
            down = jnp.where(lane_all == 0, 0.0, pltpu.roll(part[2 * ROWS :], 1, 1))
            ss[pl.ds(pl.multiple_of(col * ROWS, ROWS), ROWS), :] = part[:ROWS] + up + down
            part = rk[:, 128 * half : 128 * half + 128]
            up = jnp.where(lane48 == 127, 0.0, pltpu.roll(part[48:96], 127, 1))
            down = jnp.where(lane48 == 0, 0.0, pltpu.roll(part[96:], 1, 1))
            sgk[pl.ds(pl.multiple_of(col * 48, 48), 48), :] = part[:48] + up + down
        return carry

    lax.fori_loop(0, 16, pair, 0, unroll=UNROLL_S)

    pl.when(high_ok)(to_low.wait_recv)
    pl.when(low_ok)(to_high.wait_recv)
    lane = lax.broadcasted_iota(jnp.int32, (32, 128), 1)
    k_low = jnp.where(low_ok, gin[0, 0:32, :], 0.0)
    k_high = jnp.where(high_ok, gin[1, 0:32, :], 0.0)
    lane96 = lax.broadcasted_iota(jnp.int32, (96, 128), 1)

    def spread(packed):
        return jnp.concatenate(
            [packed if k == 0 else pltpu.roll(packed, 128 - 32 * k, 1) for k in range(4)], axis=0)

    h_high = spread(jnp.where(high_ok, gin[1, 32:56, :], 0.0))
    h_low = spread(jnp.where(low_ok, gin[0, 32:56, :], 0.0))
    kc_high = jnp.concatenate([k_high[:, 0:1]] * 3, axis=0)
    kc_low = jnp.concatenate([k_low[:, 127:128]] * 3, axis=0)
    edges = jnp.where(lane96 < 32, h_high, pltpu.roll(h_low, 32, 1))
    kedges = jnp.where(lane96 < 32, h_high * kc_high, pltpu.roll(h_low * kc_low, 32, 1))
    edges = jnp.where(lane96 < 64, edges, pltpu.roll(kedges, 64, 1))
    ch = dot(c_all[...], split(edges))

    for p, r, copy in halo:
        pl.when(inside(-p, -r))(copy.wait_recv)
    ke[...] = jnp.zeros_like(ke)
    for x in range(4):
        ke[1 + x, 1:9, :] = ks[8 * x : 8 * x + 8, :]
        ke[1 + x, 0:1, :] = jnp.where(inside(0, -1), khy[0, x : 1 + x, :], 0.0)
        ke[1 + x, 9:10, :] = jnp.where(inside(0, 1), khy[1, x : 1 + x, :], 0.0)
    ke[0, 1:9, :] = jnp.where(inside(-1, 0), khx[0], 0.0)
    ke[5, 1:9, :] = jnp.where(inside(1, 0), khx[1], 0.0)
    ke[0, 0:1, :] = jnp.where(inside(-1, -1), khc[0, 3:4, :], 0.0)
    ke[0, 9:10, :] = jnp.where(inside(-1, 1), khc[1, 3:4, :], 0.0)
    ke[5, 0:1, :] = jnp.where(inside(1, -1), khc[2, 0:1, :], 0.0)
    ke[5, 9:10, :] = jnp.where(inside(1, 1), khc[3, 0:1, :], 0.0)
    strips = [ke[x, 1:9, :] + 0.5 * (ke[x, 0:8, :] + ke[x, 2:10, :]) for x in range(6)]
    smooth = jnp.concatenate([strips[x + 1] + 0.5 * (strips[x] + strips[x + 2]) for x in range(4)], axis=0)
    up = jnp.where(lane == 127, 0.0, pltpu.roll(smooth, 127, 1))
    down = jnp.where(lane == 0, 0.0, pltpu.roll(smooth, 1, 1))
    kd[...] = 228.0 * ks[...] + 36.0 * smooth + 18.0 * (up + down)
    for a in range(3):
        kt[8 * a : 8 * a + 8, :] = khx[1]
        for x in range(4):
            kt[24 + 3 * x + a : 25 + 3 * x + a, :] = khy[1, x : x + 1, :]
        kt[36 + a : 37 + a, :] = khc[3, 0:1, :]
        kt[39 + a : 40 + a, :] = khc[2, 0:1, :]
    kt[42:48, :] = jnp.zeros((6, 128), F32)

    def column(tile, at):
        return jnp.concatenate([tile[:, at : at + 1]] * 3, axis=0)

    own_low = spread(gout[0, 32:56, :])
    own_high = spread(gout[1, 32:56, :])
    left = jnp.concatenate([
        h_low * (18.0 * column(smooth, 0)), h_high * (18.0 * column(smooth, 127)),
        -own_high * column(kappa, 127), -own_low * column(kappa, 0)], axis=0)
    right = jnp.concatenate([
        h_low, h_high, ch[ROWS : ROWS + 96], pltpu.roll(ch[2 * ROWS : 2 * ROWS + 96], 96, 1)], axis=0)
    outside = dot_tn(left, right)[:32, :32]

    g_high = ch[ROWS + 96 : 2 * ROWS]
    g_low = ch[2 * ROWS + 96 :]
    g_high = kt[:, 127:128] * g_high + pltpu.roll(g_high, 64, 1)
    g_low = kt[:, 0:1] * g_low + pltpu.roll(g_low, 64, 1)
    turn = jnp.where(lane48 < 32, g_high, g_low).T
    turn_high = jnp.concatenate([turn[0:32], jnp.zeros((32, 80), F32)], axis=1)
    turn_low = jnp.concatenate([turn[32:64], jnp.zeros((32, 80), F32)], axis=1)

    def ghost(step, carry):
        tiles = []
        for y in range(8):
            m = step * 8 + y
            tile = kt[pl.ds(m, 1), :] * ss[pl.ds(96 + m, 32, stride=ROWS), :] + sgk[pl.ds(m, 32, stride=48), :]
            high = jnp.where(lane == 127, pltpu.roll(turn_high, 127 - m, 1), 0.0)
            tile = tile + jnp.where(lane == 0, pltpu.roll(turn_low, lax.rem(128 - m, 128), 1), high)
            qg[m] = tile
            tiles.append(tile)
        qb[:, pl.ds(pl.multiple_of(step * 1024, 1024), 1024)] = split(jnp.concatenate(tiles, axis=1))
        return carry

    lax.fori_loop(0, 6, ghost, 0)
    corners = [
        (0, 1, remote(qg.at[pl.ds(36, 3)], qc.at[0], cs.at[0], cr.at[0], near(0, 1), g)),
        (0, -1, remote(qg.at[pl.ds(39, 3)], qc.at[1], cs.at[1], cr.at[1], near(0, -1), g)),
    ]
    for p, r, copy in corners:
        pl.when(inside(p, r))(copy.start)

    @pl.when(g < SLABS - 2)
    def _():
        pl.semaphore_wait(hello.at[1], SLABS - 2 - g)

    heard = jnp.int32(0)
    for p, r in ((1, 0), (0, 1), (0, -1)):
        heard = heard + inside(p, r).astype(jnp.int32)

        @pl.when(inside(-p, -r))
        def _():
            pl.semaphore_signal(ready, inc=1, device_id={"sub": near(-p, -r), "grp": g}, device_id_type=MESH)

    def inner(step, total):
        start_z = (step // 4) * 1024 + lax.rem(step, 4) * 8
        start_s = step * 8
        start_k = lax.rem(step, 4) * 8
        left, right = [], []
        for y in range(8):
            z = zs[pl.ds(start_z + y, 32, stride=32), :]
            v = ss[pl.ds(start_s + y, 32, stride=ROWS), :]
            left.append(z)
            right.append(kd[pl.ds(start_k + y, 1), :] * z - ks[pl.ds(start_k + y, 1), :] * v)
        left = split(jnp.concatenate(left, axis=1))
        right = split(jnp.concatenate(right, axis=1))
        return total + dot_nt(left, right)

    total = quadrants(lax.fori_loop(0, 12, inner, jnp.zeros((64, 64), F32), unroll=UNROLL_N)) + outside
    total = (total + total.T) * (1.0 / 48.0)
    nin[g, :, 0:32] = total
    sums = [remote(nin.at[g], nin.at[g], ns.at[d - 1], nr.at[d - 1], s, slab(d)) for d in (1, 2, 3)]
    for copy in sums:
        copy.start()

    flat = rx.reshape(768, 128)

    def face(a):
        return split(jnp.concatenate([flat[pl.ds(a * 256 + y, 32, stride=8), :] for y in range(8)], axis=1))

    lane32 = lax.broadcasted_iota(jnp.int32, (32, 128), 1)
    lane8 = lax.broadcasted_iota(jnp.int32, (8, 128), 1)

    def pack(block):
        wide = jnp.concatenate([block, jnp.zeros((32, 96), F32)], axis=1)
        result = wide[0:8]
        for k in range(1, 4):
            result = jnp.where(lane8 // 32 == k, pltpu.roll(wide[8 * k : 8 * k + 8], 32 * k, 1), result)
        return result

    def scaled(value, ok):
        return jnp.where(ok, quadrants(value) * (-1.0 / 48.0), 0.0)

    sent = []

    def give(src, slot, count, p, r, which, slabs):
        for d in slabs:
            copy = remote(src, inbox.at[g, pl.ds(slot, count)], bs.at[which, d], br.at[which, d], near(p, r), slab(d))
            pl.when(inside(p, r))(copy.start)
            sent.append((p, r, copy))

    pl.semaphore_wait(ready, heard)

    pl.when(inside(0, 1))(faces[3][2].wait_recv)
    block = scaled(dot_nt(qb[:, 24 * 128 : 36 * 128], split(jnp.concatenate([ry[t] for t in range(12)], axis=1))), inside(0, 1))
    inbox[g, 4] = pack(block)
    outbox[0] = pack(block.T)
    give(inbox.at[g, pl.ds(4, 1)], 4, 1, 0, 0, 0, (1, 2, 3))
    give(outbox.at[pl.ds(0, 1)], 3, 1, 0, 1, 1, range(4))

    for p, r, copy in corners:
        pl.when(inside(-p, -r))(copy.wait_recv)
    side = [split(jnp.concatenate([qc[e, a] for a in range(3)], axis=1)) for e in range(2)]
    value = jnp.zeros((64, 64), F32)
    value_low = jnp.zeros((64, 64), F32)
    value_high = jnp.zeros((64, 64), F32)
    for a in range(3):
        pl.when(inside(1, 0))(faces[a][2].wait_recv)
        f = face(a)
        value = value + dot_nt(qb[:, a * 1024 : (a + 1) * 1024], f)
        value_low = value_low + dot_nt(side[0][:, 128 * a : 128 * a + 128], f[:, 0:128])
        value_high = value_high + dot_nt(side[1][:, 128 * a : 128 * a + 128], f[:, 896:1024])
    block = scaled(value, inside(1, 0))
    block_low = scaled(value_low, inside(1, -1))
    block_high = scaled(value_high, inside(1, 1))
    outbox[1] = pack(block_low.T)
    outbox[2] = pack(block.T)
    outbox[3] = pack(block_high.T)
    give(outbox.at[pl.ds(1, 3)], 0, 3, 1, 0, 2, range(4))
    outbox[4] = pack(block_low)
    give(outbox.at[pl.ds(4, 1)], 7, 1, 0, -1, 3, range(4))
    outbox[5] = pack(block_high)
    give(outbox.at[pl.ds(5, 1)], 5, 1, 0, 1, 4, range(4))
    inbox[g, 6] = pack(block)
    give(inbox.at[g, pl.ds(6, 1)], 6, 1, 0, 0, 5, (1, 2, 3))

    for copy in sums:
        copy.wait_recv()
    row32 = lax.broadcasted_iota(jnp.int32, (32, 128), 0)
    m = nin[0] + nin[1] + nin[2] + nin[3]
    m = jnp.where(lane32 < 32, m, jnp.where(lane32 == row32 + 32, 1.0, 0.0))
    lower = jnp.zeros((32, 128), F32)
    for k in range(32):
        pivot = m[k : k + 1, k : k + 1]
        r = lax.rsqrt(pivot)
        r = r * (1.5 - 0.5 * pivot * r * r)
        col = m[:, k : k + 1] * r
        line = m[k : k + 1, :] * r
        lower = jnp.where(jnp.logical_and(lane32 == k, row32 >= k), col, lower)
        m = jnp.where(row32 > k, m - col * line, jnp.where(row32 == k, line, m))
    factor[...] = lower[:, 0:32] * (1.0 / np.sqrt(49152.0))
    inverse = m[:, 32:64]

    for p, r, copy in sent:
        pl.when(inside(-p, -r))(copy.wait_recv)
    packed = [jnp.where(inside(*ALL_NEAR[b]), inbox[0, b] + inbox[1, b] + inbox[2, b] + inbox[3, b], 0.0) for b in range(8)]
    halves = []
    for part in range(2):
        rows = []
        for k in range(4):
            result = jnp.zeros((8, 128), F32)
            for at in range(4):
                shift = (32 * (at - k)) % 128
                moved = packed[4 * part + at]
                moved = moved if shift == 0 else pltpu.roll(moved, shift, 1)
                result = jnp.where(lane8 // 32 == at, moved, result)
            rows.append(result)
        halves.append(jnp.concatenate(rows, axis=0))
    every = jnp.concatenate(halves, axis=1)
    panel[...] = lax.dot_general(inverse, every, (((1,), (0,)), ((), ())), precision=lax.Precision.HIGHEST,
                                 preferred_element_type=F32)

    pl.when(low_ok)(to_low.wait_send)
    pl.when(high_ok)(to_high.wait_send)
    for copy in sums:
        copy.wait_send()
    for p, r, copy in halo + sent:
        pl.when(inside(p, r))(copy.wait_send)
    for p, r, copy in faces:
        pl.when(inside(-p, -r))(copy.wait_send)
    for p, r, copy in corners:
        pl.when(inside(p, r))(copy.wait_send)


def shards(stencil, basis, material, kappa_table):
    hbm = pl.BlockSpec(memory_space=pltpu.HBM)
    vmem = pl.BlockSpec(memory_space=pltpu.VMEM)
    dma = pltpu.SemaphoreType.DMA
    operands = (basis.reshape(3072, 128), basis.reshape(96, 32, 128), material.reshape(32, 128), kappa_table, stencil)
    factor, panel = pl.pallas_call(
        kernel,
        out_shape=(jax.ShapeDtypeStruct((32, 32), F32), jax.ShapeDtypeStruct((32, 256), F32)),
        in_specs=[hbm] * 5,
        out_specs=(vmem, vmem),
        scratch_shapes=[
            pltpu.VMEM((3072, 128), F32),
            pltpu.VMEM((32, 128), jnp.int32),
            pltpu.VMEM((3 * ROWS, 192), BF16),
            pltpu.VMEM((12, 32, 128), F32),
            pltpu.VMEM((96, 8, 128), F32),
            pltpu.VMEM((12, 32, 128), F32),
            pltpu.VMEM((32, 128), F32),
            pltpu.VMEM((2, 8, 128), F32),
            pltpu.VMEM((2, 56, 128), F32),
            pltpu.VMEM((2, 56, 128), F32),
            pltpu.VMEM((2, 8, 128), F32),
            pltpu.VMEM((2, 8, 128), F32),
            pltpu.VMEM((4, 8, 128), F32),
            pltpu.VMEM((6, 16, 128), F32),
            pltpu.VMEM((32, 128), F32),
            pltpu.VMEM((48, 128), F32),
            pltpu.VMEM((96, 128), F32),
            pltpu.VMEM((32 * ROWS, 128), F32),
            pltpu.VMEM((32 * 48, 128), F32),
            pltpu.VMEM((64, 6 * 1024), BF16),
            pltpu.VMEM((48, 32, 128), F32),
            pltpu.VMEM((2, 3, 32, 128), F32),
            pltpu.VMEM((4, 32, 128), F32),
            pltpu.VMEM((4, 8, 8, 128), F32),
            pltpu.VMEM((6, 8, 128), F32),
            pltpu.SMEM((8,), F32),
            pltpu.VMEM((3 * ROWS, 192), F32),
            pltpu.SemaphoreType.REGULAR((2,)), pltpu.SemaphoreType.REGULAR,
            dma((4,)), dma((2,)), dma((2,)), dma((8,)), dma((8,)), dma((4,)), dma((4,)), dma((2,)), dma((2,)),
            dma((3,)), dma((3,)), dma((6, 4)), dma((6, 4)),
        ],
        compiler_params=pltpu.CompilerParams(
            collective_id=0, has_side_effects=True, vmem_limit_bytes=40 * 2**20),
        name="coarse_blocks",
    )(*(pltpu.with_memory_space_constraint(value, pltpu.HBM) for value in operands))
    panel = panel.reshape(32, 8, 32).transpose(1, 0, 2)
    return factor[None], panel[None]


def solution(mesh):
    placed = (P(), P("sub", None, None, None, None, "grp"), P("sub", None, None, "grp"), P())
    call = jax.shard_map(
        shards,
        mesh=mesh,
        in_specs=placed,
        out_specs=(P("sub", None, None), P("sub", None, None, None)),
        check_vma=False,
    )
    matrix = stencil_matrix()

    def run(basis, material, kappa_table):
        return call(jnp.asarray(matrix, F32), basis, material, kappa_table)

    return run
```

```python
import functools

import jax
import jax.numpy as jnp
import numpy as np
from jax import lax
from jax.experimental import pallas as pl
from jax.experimental.pallas import tpu as pltpu
from jax.sharding import PartitionSpec as P

YDOMS = 4
XDOMS = 16
SLABS = 4
MESH = pl.DeviceIdType.MESH
F32 = jnp.float32
BF16 = jnp.bfloat16
GHOSTS = 42
ROWS = 144
ALL_NEAR = [(p, r) for p in (-1, 0, 1) for r in (-1, 0, 1) if (p, r) != (0, 0)]
UNROLL_E = 8
UNROLL_S = 2
UNROLL_N = 2


def out_cells():
    cells = [(a, x, y) for a in range(3) for x in range(4) for y in range(8)]
    cells += [(a, 4, y) for a in range(3) for y in range(8)]
    cells += [(a, x, 8) for x in range(4) for a in range(3)]
    cells += [(a, 4, 8) for a in range(3)]
    cells += [(a, 4, -1) for a in range(3)]
    return cells


def stencil_matrix():
    whole = np.zeros((3, ROWS, 96), np.float64)
    for part, step_z in enumerate((0, 1, -1)):
        for row, (a, x, y) in enumerate(out_cells()):
            for p in (-1, 0, 1):
                for r in (-1, 0, 1):
                    o = (p, r, step_z)
                    q = sum(v * v for v in o)
                    if q == 0 or not (0 <= x + p < 4 and 0 <= y + r < 8):
                        continue
                    for b in range(3):
                        g = (1.0 if a == b else 0.0) + 0.5 / q * o[a] * o[b]
                        whole[part, row, b * 32 + (x + p) * 8 + y + r] += 24.0 * 0.5 ** (q - 1) * g
    whole = np.round(whole).reshape(3 * ROWS, 96)
    return np.concatenate([whole, whole], axis=1)


def split(value):
    high = value.astype(BF16)
    low = (value - high.astype(F32)).astype(BF16)
    return jnp.concatenate([high, low], axis=0)


def dot(a, b):
    return lax.dot_general(a, b, (((1,), (0,)), ((), ())), preferred_element_type=F32)


def dot_nt(a, b):
    return lax.dot_general(a, b, (((1,), (1,)), ((), ())), preferred_element_type=F32)


def dot_tn(a, b):
    return lax.dot_general(a, b, (((0,), (0,)), ((), ())), precision=lax.Precision.HIGHEST, preferred_element_type=F32)


def quadrants(r):
    top = r[:32] + r[32:]
    return top[:, :32] + top[:, 32:]


def kernel(basis, planes, material, table, stencil, factor, panel,
           zs, mat, c_all, fb, rx, ry, ks, packy, gin, gout, khx, khy, khc, ke, kd, kt, k3,
           ss, sgk, qb, qg, qc, nin, inbox, outbox, tab, c_in,
           hello, ready, lsem, gs, gr, hs, hr, fs, fr, cs, cr, ns, nr, bs, br):
    s = lax.axis_index("sub")
    g = lax.axis_index("grp")
    i = s // YDOMS
    j = lax.rem(s, YDOMS)

    def near(p, r):
        return lax.rem(i + p + XDOMS, XDOMS) * YDOMS + lax.rem(j + r + YDOMS, YDOMS)

    def inside(p, r):
        ok = i >= 0
        if p:
            ok = jnp.logical_and(ok, i < XDOMS - 1 if p > 0 else i > 0)
        if r:
            ok = jnp.logical_and(ok, j < YDOMS - 1 if r > 0 else j > 0)
        return ok

    def slab(d):
        return lax.rem(g + d + SLABS, SLABS)

    def remote(src, dst, send, recv, sub, grp):
        return pltpu.make_async_remote_copy(
            src_ref=src, dst_ref=dst, send_sem=send, recv_sem=recv,
            device_id={"sub": sub, "grp": grp}, device_id_type=MESH)

    barrier = pltpu.get_barrier_semaphore()
    entered = g
    for p, r in ALL_NEAR:
        entered = entered + inside(p, r).astype(jnp.int32)

        @pl.when(inside(p, r))
        def _():
            pl.semaphore_signal(barrier, inc=1, device_id={"sub": near(p, r), "grp": g}, device_id_type=MESH)

    for d in (1, 2, 3):

        @pl.when(g + d < SLABS)
        def _():
            pl.semaphore_signal(barrier, inc=1, device_id={"sub": s, "grp": slab(d)}, device_id_type=MESH)

    load_mat = pltpu.make_async_copy(material, mat, lsem.at[0])
    load_zs = pltpu.make_async_copy(basis, zs, lsem.at[1])
    load_c = pltpu.make_async_copy(stencil, c_in, lsem.at[2])
    load_tab = pltpu.make_async_copy(table, tab, lsem.at[3])
    load_mat.start()
    load_tab.start()
    load_zs.start()
    load_c.start()

    load_mat.wait()
    load_tab.wait()
    ids = mat[...]
    kappa = jnp.zeros((32, 128), F32)
    for which in range(8):
        kappa = kappa + jnp.where(ids == which, tab[which], 0.0)
    ks[...] = kappa
    for e, y in ((0, 0), (1, 7)):
        for x in range(4):
            packy[e, x : x + 1, :] = ks[8 * x + y : 8 * x + y + 1, :]
    for a in range(3):
        k3[32 * a : 32 * a + 32, :] = kappa
    lane8 = lax.broadcasted_iota(jnp.int32, (8, 128), 1)

    def fold(wide):
        result = wide[0:8]
        for k in range(1, 4):
            result = jnp.where(lane8 // 32 == k, pltpu.roll(wide[8 * k : 8 * k + 8], 32 * k, 1), result)
        return result

    def spread(packed):
        return jnp.concatenate(
            [packed if k == 0 else pltpu.roll(packed, 128 - 32 * k, 1) for k in range(4)], axis=0)

    gout[0, 0:8, :] = fold(kappa)
    gout[1, 0:8, :] = fold(pltpu.roll(kappa, 1, 1))

    load_zs.wait()
    for x in range(4):
        for a in range(3):
            fb[3 * x + a] = zs[pl.ds(a * 1024 + x * 8, 32, stride=32), :]
    pl.semaphore_wait(barrier, entered)
    for d in (1, 2, 3):

        @pl.when(g >= d)
        def _():
            pl.semaphore_signal(hello.at[min(d, 2) - 1], inc=1, device_id={"sub": s, "grp": slab(-d)}, device_id_type=MESH)

    halo = [
        (-1, 0, remote(ks.at[pl.ds(0, 8)], khx.at[1], hs.at[0], hr.at[0], near(-1, 0), g)),
        (1, 0, remote(ks.at[pl.ds(24, 8)], khx.at[0], hs.at[1], hr.at[1], near(1, 0), g)),
        (0, -1, remote(packy.at[0], khy.at[1], hs.at[2], hr.at[2], near(0, -1), g)),
        (0, 1, remote(packy.at[1], khy.at[0], hs.at[3], hr.at[3], near(0, 1), g)),
        (-1, -1, remote(packy.at[0], khc.at[3], hs.at[4], hr.at[4], near(-1, -1), g)),
        (1, 1, remote(packy.at[1], khc.at[0], hs.at[5], hr.at[5], near(1, 1), g)),
        (-1, 1, remote(packy.at[1], khc.at[2], hs.at[6], hr.at[6], near(-1, 1), g)),
        (1, -1, remote(packy.at[0], khc.at[1], hs.at[7], hr.at[7], near(1, -1), g)),
    ]
    for p, r, copy in halo:
        pl.when(inside(p, r))(copy.start)
    faces = [
        (1, 0, remote(planes.at[pl.ds(32 * a, 32), pl.ds(0, 8)], rx.at[pl.ds(32 * a, 32)], fs.at[a], fr.at[a], near(-1, 0), g))
        for a in range(3)
    ]
    faces.append((0, 1, remote(fb, ry, fs.at[3], fr.at[3], near(0, -1), g)))
    for p, r, copy in faces[3:] + faces[:1]:
        pl.when(inside(-p, -r))(copy.start)
    lane24 = lax.broadcasted_iota(jnp.int32, (24, 128), 1)

    def own(col):
        return jnp.concatenate(
            [zs[pl.ds(pl.multiple_of(a * 1024 + col * 32, 32), 32), :] for a in range(3)], axis=0)

    def edge(col, carry):
        first, last = carry
        u = own(col)
        for k in range(4):
            rows = u[24 * k : 24 * k + 24]
            here = lane24 == 32 * k + col
            first = jnp.where(here, pltpu.roll(rows, 32 * k + col, 1), first)
            last = jnp.where(here, pltpu.roll(rows, lax.rem(32 * k + col + 1, 128), 1), last)
        return first, last

    zero24 = jnp.zeros((24, 128), F32)
    first, last = lax.fori_loop(0, 32, edge, (zero24, zero24), unroll=UNROLL_E)
    gout[0, 8:32, :] = first
    gout[1, 8:32, :] = last

    to_low = remote(gout.at[0], gin.at[1], gs.at[0], gr.at[1], s, slab(-1))
    to_high = remote(gout.at[1], gin.at[0], gs.at[1], gr.at[0], s, slab(1))
    low_ok = g > 0
    high_ok = g < SLABS - 1
    pl.when(low_ok)(to_low.start)

    @pl.when(high_ok)
    def _():
        pl.semaphore_wait(hello.at[0], 1)
        to_high.start()

    for p, r, copy in faces[1:3]:
        pl.when(inside(-p, -r))(copy.start)
    load_c.wait()
    c_all[...] = c_in[...].astype(BF16)
    kpair = jnp.concatenate([k3[...], k3[...]], axis=1)
    c_ghost = jnp.concatenate([c_all[part * ROWS + 96 : (part + 1) * ROWS, :] for part in range(3)], axis=0)
    lane_all = lax.broadcasted_iota(jnp.int32, (ROWS, 128), 1)
    lane48 = lax.broadcasted_iota(jnp.int32, (48, 128), 1)

    def pair(step, carry):
        u = jnp.concatenate([own(2 * step), own(2 * step + 1)], axis=1)
        r = dot(c_all[...], split(u))
        rk = dot(c_ghost, split(u * kpair))
        for half in range(2):
            col = 2 * step + half
            part = r[:, 128 * half : 128 * half + 128]
            up = jnp.where(lane_all == 127, 0.0, pltpu.roll(part[ROWS : 2 * ROWS], 127, 1))
            down = jnp.where(lane_all == 0, 0.0, pltpu.roll(part[2 * ROWS :], 1, 1))
            ss[pl.ds(pl.multiple_of(col * ROWS, ROWS), ROWS), :] = part[:ROWS] + up + down
            part = rk[:, 128 * half : 128 * half + 128]
            up = jnp.where(lane48 == 127, 0.0, pltpu.roll(part[48:96], 127, 1))
            down = jnp.where(lane48 == 0, 0.0, pltpu.roll(part[96:], 1, 1))
            sgk[pl.ds(pl.multiple_of(col * 48, 48), 48), :] = part[:48] + up + down
        return carry

    lax.fori_loop(0, 16, pair, 0, unroll=UNROLL_S)

    pl.when(high_ok)(to_low.wait_recv)
    pl.when(low_ok)(to_high.wait_recv)
    lane = lax.broadcasted_iota(jnp.int32, (32, 128), 1)
    lane96 = lax.broadcasted_iota(jnp.int32, (96, 128), 1)

    h_high = spread(jnp.where(high_ok, gin[1, 8:32, :], 0.0))
    h_low = spread(jnp.where(low_ok, gin[0, 8:32, :], 0.0))
    kc_high = jnp.concatenate([spread(jnp.where(high_ok, gin[1, 0:8, :], 0.0))[:, 0:1]] * 3, axis=0)
    kc_low = jnp.concatenate([spread(jnp.where(low_ok, gin[0, 0:8, :], 0.0))[:, 0:1]] * 3, axis=0)
    edges = jnp.where(lane96 < 32, h_high, pltpu.roll(h_low, 32, 1))
    kedges = jnp.where(lane96 < 32, h_high * kc_high, pltpu.roll(h_low * kc_low, 32, 1))
    edges = jnp.where(lane96 < 64, edges, pltpu.roll(kedges, 64, 1))
    ch = dot(c_all[...], split(edges))

    for p, r, copy in halo:
        pl.when(inside(-p, -r))(copy.wait_recv)
    ke[...] = jnp.zeros_like(ke)
    for x in range(4):
        ke[1 + x, 1:9, :] = ks[8 * x : 8 * x + 8, :]
        ke[1 + x, 0:1, :] = jnp.where(inside(0, -1), khy[0, x : 1 + x, :], 0.0)
        ke[1 + x, 9:10, :] = jnp.where(inside(0, 1), khy[1, x : 1 + x, :], 0.0)
    ke[0, 1:9, :] = jnp.where(inside(-1, 0), khx[0], 0.0)
    ke[5, 1:9, :] = jnp.where(inside(1, 0), khx[1], 0.0)
    ke[0, 0:1, :] = jnp.where(inside(-1, -1), khc[0, 3:4, :], 0.0)
    ke[0, 9:10, :] = jnp.where(inside(-1, 1), khc[1, 3:4, :], 0.0)
    ke[5, 0:1, :] = jnp.where(inside(1, -1), khc[2, 0:1, :], 0.0)
    ke[5, 9:10, :] = jnp.where(inside(1, 1), khc[3, 0:1, :], 0.0)
    strips = [ke[x, 1:9, :] + 0.5 * (ke[x, 0:8, :] + ke[x, 2:10, :]) for x in range(6)]
    smooth = jnp.concatenate([strips[x + 1] + 0.5 * (strips[x] + strips[x + 2]) for x in range(4)], axis=0)
    up = jnp.where(lane == 127, 0.0, pltpu.roll(smooth, 127, 1))
    down = jnp.where(lane == 0, 0.0, pltpu.roll(smooth, 1, 1))
    kd[...] = 228.0 * ks[...] + 36.0 * smooth + 18.0 * (up + down)
    for a in range(3):
        kt[8 * a : 8 * a + 8, :] = khx[1]
        for x in range(4):
            kt[24 + 3 * x + a : 25 + 3 * x + a, :] = khy[1, x : x + 1, :]
        kt[36 + a : 37 + a, :] = khc[3, 0:1, :]
        kt[39 + a : 40 + a, :] = khc[2, 0:1, :]
    kt[42:48, :] = jnp.zeros((6, 128), F32)

    def column(tile, at):
        return jnp.concatenate([tile[:, at : at + 1]] * 3, axis=0)

    own_low = spread(gout[0, 8:32, :])
    own_high = spread(gout[1, 8:32, :])
    left = jnp.concatenate([
        h_low * (18.0 * column(smooth, 0)), h_high * (18.0 * column(smooth, 127)),
        -own_high * column(kappa, 127), -own_low * column(kappa, 0)], axis=0)
    right = jnp.concatenate([
        h_low, h_high, ch[ROWS : ROWS + 96], pltpu.roll(ch[2 * ROWS : 2 * ROWS + 96], 96, 1)], axis=0)
    outside = dot_tn(left, right)[:32, :32]

    g_high = ch[ROWS + 96 : 2 * ROWS]
    g_low = ch[2 * ROWS + 96 :]
    g_high = kt[:, 127:128] * g_high + pltpu.roll(g_high, 64, 1)
    g_low = kt[:, 0:1] * g_low + pltpu.roll(g_low, 64, 1)
    turn = jnp.where(lane48 < 32, g_high, g_low).T
    turn_high = jnp.concatenate([turn[0:32], jnp.zeros((32, 80), F32)], axis=1)
    turn_low = jnp.concatenate([turn[32:64], jnp.zeros((32, 80), F32)], axis=1)

    def ghost(step, carry):
        tiles = []
        for y in range(8):
            m = step * 8 + y
            tile = kt[pl.ds(m, 1), :] * ss[pl.ds(96 + m, 32, stride=ROWS), :] + sgk[pl.ds(m, 32, stride=48), :]
            high = jnp.where(lane == 127, pltpu.roll(turn_high, 127 - m, 1), 0.0)
            tile = tile + jnp.where(lane == 0, pltpu.roll(turn_low, lax.rem(128 - m, 128), 1), high)
            qg[m] = tile
            tiles.append(tile)
        qb[:, pl.ds(pl.multiple_of(step * 1024, 1024), 1024)] = split(jnp.concatenate(tiles, axis=1))
        return carry

    lax.fori_loop(0, 6, ghost, 0)
    corners = [
        (0, 1, remote(qg.at[pl.ds(36, 3)], qc.at[0], cs.at[0], cr.at[0], near(0, 1), g)),
        (0, -1, remote(qg.at[pl.ds(39, 3)], qc.at[1], cs.at[1], cr.at[1], near(0, -1), g)),
    ]
    for p, r, copy in corners:
        pl.when(inside(p, r))(copy.start)

    @pl.when(g < SLABS - 2)
    def _():
        pl.semaphore_wait(hello.at[1], SLABS - 2 - g)

    heard = jnp.int32(0)
    for p, r in ((1, 0), (0, 1), (0, -1)):
        heard = heard + inside(p, r).astype(jnp.int32)

        @pl.when(inside(-p, -r))
        def _():
            pl.semaphore_signal(ready, inc=1, device_id={"sub": near(-p, -r), "grp": g}, device_id_type=MESH)

    def inner(step, total):
        start_z = (step // 4) * 1024 + lax.rem(step, 4) * 8
        start_s = step * 8
        start_k = lax.rem(step, 4) * 8
        left, right = [], []
        for y in range(8):
            z = zs[pl.ds(start_z + y, 32, stride=32), :]
            v = ss[pl.ds(start_s + y, 32, stride=ROWS), :]
            left.append(z)
            right.append(kd[pl.ds(start_k + y, 1), :] * z - ks[pl.ds(start_k + y, 1), :] * v)
        left = split(jnp.concatenate(left, axis=1))
        right = split(jnp.concatenate(right, axis=1))
        return total + dot_nt(left, right)

    total = quadrants(lax.fori_loop(0, 12, inner, jnp.zeros((64, 64), F32), unroll=UNROLL_N)) + outside
    total = (total + total.T) * (1.0 / 48.0)
    nin[g, :, 0:32] = total
    sums = [remote(nin.at[g], nin.at[g], ns.at[d - 1], nr.at[d - 1], s, slab(d)) for d in (1, 2, 3)]
    for copy in sums:
        copy.start()

    flat = rx.reshape(768, 128)

    def face(a):
        return split(jnp.concatenate([flat[pl.ds(a * 256 + y, 32, stride=8), :] for y in range(8)], axis=1))

    lane32 = lax.broadcasted_iota(jnp.int32, (32, 128), 1)
    def pack(block):
        return fold(jnp.concatenate([block, jnp.zeros((32, 96), F32)], axis=1))

    def scaled(value, ok):
        return jnp.where(ok, quadrants(value) * (-1.0 / 48.0), 0.0)

    sent = []

    def give(src, slot, count, p, r, which, slabs):
        for d in slabs:
            copy = remote(src, inbox.at[g, pl.ds(slot, count)], bs.at[which, d], br.at[which, d], near(p, r), slab(d))
            pl.when(inside(p, r))(copy.start)
            sent.append((p, r, copy))

    pl.semaphore_wait(ready, heard)

    pl.when(inside(0, 1))(faces[3][2].wait_recv)
    block = scaled(dot_nt(qb[:, 24 * 128 : 36 * 128], split(jnp.concatenate([ry[t] for t in range(12)], axis=1))), inside(0, 1))
    inbox[g, 4] = pack(block)
    outbox[0] = pack(block.T)
    give(inbox.at[g, pl.ds(4, 1)], 4, 1, 0, 0, 0, (1, 2, 3))
    give(outbox.at[pl.ds(0, 1)], 3, 1, 0, 1, 1, range(4))

    for p, r, copy in corners:
        pl.when(inside(-p, -r))(copy.wait_recv)
    side = [split(jnp.concatenate([qc[e, a] for a in range(3)], axis=1)) for e in range(2)]
    value = jnp.zeros((64, 64), F32)
    value_low = jnp.zeros((64, 64), F32)
    value_high = jnp.zeros((64, 64), F32)
    for a in range(3):
        pl.when(inside(1, 0))(faces[a][2].wait_recv)
        f = face(a)
        value = value + dot_nt(qb[:, a * 1024 : (a + 1) * 1024], f)
        value_low = value_low + dot_nt(side[0][:, 128 * a : 128 * a + 128], f[:, 0:128])
        value_high = value_high + dot_nt(side[1][:, 128 * a : 128 * a + 128], f[:, 896:1024])
    block = scaled(value, inside(1, 0))
    block_low = scaled(value_low, inside(1, -1))
    block_high = scaled(value_high, inside(1, 1))
    inbox[g, 6] = pack(block)
    outbox[1] = pack(block_low.T)
    outbox[2] = pack(block.T)
    outbox[3] = pack(block_high.T)
    outbox[4] = pack(block_low)
    outbox[5] = pack(block_high)
    give(outbox.at[pl.ds(1, 3)], 0, 3, 1, 0, 2, (2, 3, 1, 0))
    give(inbox.at[g, pl.ds(6, 1)], 6, 1, 0, 0, 5, (2, 3, 1))
    give(outbox.at[pl.ds(4, 1)], 7, 1, 0, -1, 3, (2, 3, 1, 0))
    give(outbox.at[pl.ds(5, 1)], 5, 1, 0, 1, 4, (2, 3, 1, 0))

    for copy in sums:
        copy.wait_recv()
    row32 = lax.broadcasted_iota(jnp.int32, (32, 128), 0)
    m = nin[0] + nin[1] + nin[2] + nin[3]
    m = jnp.where(lane32 < 32, m, jnp.where(lane32 == row32 + 32, 1.0, 0.0))
    lower = jnp.zeros((32, 128), F32)
    for k in range(32):
        pivot = m[k : k + 1, k : k + 1]
        r = lax.rsqrt(pivot)
        r = r * (1.5 - 0.5 * pivot * r * r)
        col = m[:, k : k + 1] * r
        line = m[k : k + 1, :] * r
        lower = jnp.where(jnp.logical_and(lane32 == k, row32 >= k), col, lower)
        m = jnp.where(row32 > k, m - col * line, jnp.where(row32 == k, line, m))
    factor[...] = lower[:, 0:32] * (1.0 / np.sqrt(49152.0))
    inverse = m[:, 32:64]

    for p, r, copy in sent:
        pl.when(inside(-p, -r))(copy.wait_recv)
    packed = [jnp.where(inside(*ALL_NEAR[b]), inbox[0, b] + inbox[1, b] + inbox[2, b] + inbox[3, b], 0.0) for b in range(8)]
    halves = []
    for part in range(2):
        rows = []
        for k in range(4):
            result = jnp.zeros((8, 128), F32)
            for at in range(4):
                shift = (32 * (at - k)) % 128
                moved = packed[4 * part + at]
                moved = moved if shift == 0 else pltpu.roll(moved, shift, 1)
                result = jnp.where(lane8 // 32 == at, moved, result)
            rows.append(result)
        halves.append(jnp.concatenate(rows, axis=0))
    every = jnp.concatenate(halves, axis=1)
    solved = lax.dot_general(inverse, every, (((1,), (0,)), ((), ())), precision=lax.Precision.HIGHEST,
                             preferred_element_type=F32)
    for b in range(8):
        panel[b] = solved[:, 32 * b : 32 * b + 32]

    pl.when(low_ok)(to_low.wait_send)
    pl.when(high_ok)(to_high.wait_send)
    for copy in sums:
        copy.wait_send()
    for p, r, copy in halo + sent:
        pl.when(inside(p, r))(copy.wait_send)
    for p, r, copy in faces:
        pl.when(inside(-p, -r))(copy.wait_send)
    for p, r, copy in corners:
        pl.when(inside(p, r))(copy.wait_send)


def shards(stencil, basis, material, kappa_table):
    hbm = pl.BlockSpec(memory_space=pltpu.HBM)
    vmem = pl.BlockSpec(memory_space=pltpu.VMEM)
    dma = pltpu.SemaphoreType.DMA
    operands = (basis.reshape(3072, 128), basis.reshape(96, 32, 128), material.reshape(32, 128), kappa_table, stencil)
    factor, panel = pl.pallas_call(
        kernel,
        out_shape=(jax.ShapeDtypeStruct((32, 32), F32), jax.ShapeDtypeStruct((8, 32, 32), F32)),
        in_specs=[hbm] * 5,
        out_specs=(vmem, vmem),
        scratch_shapes=[
            pltpu.VMEM((3072, 128), F32),
            pltpu.VMEM((32, 128), jnp.int32),
            pltpu.VMEM((3 * ROWS, 192), BF16),
            pltpu.VMEM((12, 32, 128), F32),
            pltpu.VMEM((96, 8, 128), F32),
            pltpu.VMEM((12, 32, 128), F32),
            pltpu.VMEM((32, 128), F32),
            pltpu.VMEM((2, 8, 128), F32),
            pltpu.VMEM((2, 32, 128), F32),
            pltpu.VMEM((2, 32, 128), F32),
            pltpu.VMEM((2, 8, 128), F32),
            pltpu.VMEM((2, 8, 128), F32),
            pltpu.VMEM((4, 8, 128), F32),
            pltpu.VMEM((6, 16, 128), F32),
            pltpu.VMEM((32, 128), F32),
            pltpu.VMEM((48, 128), F32),
            pltpu.VMEM((96, 128), F32),
            pltpu.VMEM((32 * ROWS, 128), F32),
            pltpu.VMEM((32 * 48, 128), F32),
            pltpu.VMEM((64, 6 * 1024), BF16),
            pltpu.VMEM((48, 32, 128), F32),
            pltpu.VMEM((2, 3, 32, 128), F32),
            pltpu.VMEM((4, 32, 128), F32),
            pltpu.VMEM((4, 8, 8, 128), F32),
            pltpu.VMEM((6, 8, 128), F32),
            pltpu.SMEM((8,), F32),
            pltpu.VMEM((3 * ROWS, 192), F32),
            pltpu.SemaphoreType.REGULAR((2,)), pltpu.SemaphoreType.REGULAR,
            dma((4,)), dma((2,)), dma((2,)), dma((8,)), dma((8,)), dma((4,)), dma((4,)), dma((2,)), dma((2,)),
            dma((3,)), dma((3,)), dma((6, 4)), dma((6, 4)),
        ],
        compiler_params=pltpu.CompilerParams(
            collective_id=0, has_side_effects=True, vmem_limit_bytes=40 * 2**20),
        name="coarse_blocks",
    )(*(pltpu.with_memory_space_constraint(value, pltpu.HBM) for value in operands))
    return factor[None], panel[None]


def solution(mesh):
    placed = (P(), P("sub", None, None, None, None, "grp"), P("sub", None, None, "grp"), P())
    call = jax.shard_map(
        shards,
        mesh=mesh,
        in_specs=placed,
        out_specs=(P("sub", None, None), P("sub", None, None, None)),
        check_vma=False,
    )
    matrix = stencil_matrix()

    def run(basis, material, kappa_table):
        return call(jnp.asarray(matrix, F32), basis, material, kappa_table)

    return run
```

```python
import functools

import jax
import jax.numpy as jnp
import numpy as np
from jax import lax
from jax.experimental import pallas as pl
from jax.experimental.pallas import tpu as pltpu
from jax.sharding import PartitionSpec as P

YDOMS = 4
XDOMS = 16
SLABS = 4
MESH = pl.DeviceIdType.MESH
F32 = jnp.float32
BF16 = jnp.bfloat16
GHOSTS = 42
ROWS = 144
ALL_NEAR = [(p, r) for p in (-1, 0, 1) for r in (-1, 0, 1) if (p, r) != (0, 0)]
UNROLL_E = 8
UNROLL_S = 2
UNROLL_N = 2


def out_cells():
    cells = [(a, x, y) for a in range(3) for x in range(4) for y in range(8)]
    cells += [(a, 4, y) for a in range(3) for y in range(8)]
    cells += [(a, x, 8) for x in range(4) for a in range(3)]
    cells += [(a, 4, 8) for a in range(3)]
    cells += [(a, 4, -1) for a in range(3)]
    return cells


def stencil_matrix():
    whole = np.zeros((3, ROWS, 96), np.float64)
    for part, step_z in enumerate((0, 1, -1)):
        for row, (a, x, y) in enumerate(out_cells()):
            for p in (-1, 0, 1):
                for r in (-1, 0, 1):
                    o = (p, r, step_z)
                    q = sum(v * v for v in o)
                    if q == 0 or not (0 <= x + p < 4 and 0 <= y + r < 8):
                        continue
                    for b in range(3):
                        g = (1.0 if a == b else 0.0) + 0.5 / q * o[a] * o[b]
                        whole[part, row, b * 32 + (x + p) * 8 + y + r] += 24.0 * 0.5 ** (q - 1) * g
    whole = np.round(whole).reshape(3 * ROWS, 96)
    return np.concatenate([whole, whole], axis=1)


def split(value):
    high = value.astype(BF16)
    low = (value - high.astype(F32)).astype(BF16)
    return jnp.concatenate([high, low], axis=0)


def dot(a, b):
    return lax.dot_general(a, b, (((1,), (0,)), ((), ())), preferred_element_type=F32)


def dot_nt(a, b):
    return lax.dot_general(a, b, (((1,), (1,)), ((), ())), preferred_element_type=F32)


def dot_tn(a, b):
    return lax.dot_general(a, b, (((0,), (0,)), ((), ())), precision=lax.Precision.HIGHEST, preferred_element_type=F32)


def quadrants(r):
    top = r[:32] + r[32:]
    return top[:, :32] + top[:, 32:]


def kernel(basis, planes, material, table, stencil, factor, panel,
           zs, mat, c_all, fb, rx, ry, ks, packy, gin, gout, khx, khy, khc, ke, kd, kt, k3,
           ss, sgk, qb, qg, qc, nin, inbox, outbox, tab, c_in,
           hello, ready, lsem, gs, gr, hs, hr, fs, fr, cs, cr, ns, nr, bs, br):
    s = lax.axis_index("sub")
    g = lax.axis_index("grp")
    i = s // YDOMS
    j = lax.rem(s, YDOMS)

    def near(p, r):
        return lax.rem(i + p + XDOMS, XDOMS) * YDOMS + lax.rem(j + r + YDOMS, YDOMS)

    def inside(p, r):
        ok = i >= 0
        if p:
            ok = jnp.logical_and(ok, i < XDOMS - 1 if p > 0 else i > 0)
        if r:
            ok = jnp.logical_and(ok, j < YDOMS - 1 if r > 0 else j > 0)
        return ok

    def slab(d):
        return lax.rem(g + d + SLABS, SLABS)

    def remote(src, dst, send, recv, sub, grp):
        return pltpu.make_async_remote_copy(
            src_ref=src, dst_ref=dst, send_sem=send, recv_sem=recv,
            device_id={"sub": sub, "grp": grp}, device_id_type=MESH)

    barrier = pltpu.get_barrier_semaphore()
    entered = g
    for p, r in ALL_NEAR:
        entered = entered + inside(p, r).astype(jnp.int32)

        @pl.when(inside(p, r))
        def _():
            pl.semaphore_signal(barrier, inc=1, device_id={"sub": near(p, r), "grp": g}, device_id_type=MESH)

    for d in (1, 2, 3):

        @pl.when(g + d < SLABS)
        def _():
            pl.semaphore_signal(barrier, inc=1, device_id={"sub": s, "grp": slab(d)}, device_id_type=MESH)

    load_mat = pltpu.make_async_copy(material, mat, lsem.at[0])
    load_zs = pltpu.make_async_copy(basis, zs, lsem.at[1])
    load_c = pltpu.make_async_copy(stencil, c_in, lsem.at[2])
    load_tab = pltpu.make_async_copy(table, tab, lsem.at[3])
    load_mat.start()
    load_tab.start()
    load_zs.start()
    load_c.start()

    load_mat.wait()
    load_tab.wait()
    ids = mat[...]
    kappa = jnp.zeros((32, 128), F32)
    for which in range(8):
        kappa = kappa + jnp.where(ids == which, tab[which], 0.0)
    ks[...] = kappa
    for e, y in ((0, 0), (1, 7)):
        for x in range(4):
            packy[e, x : x + 1, :] = ks[8 * x + y : 8 * x + y + 1, :]
    for a in range(3):
        k3[32 * a : 32 * a + 32, :] = kappa
    lane8 = lax.broadcasted_iota(jnp.int32, (8, 128), 1)

    def fold(wide):
        result = wide[0:8]
        for k in range(1, 4):
            result = jnp.where(lane8 // 32 == k, pltpu.roll(wide[8 * k : 8 * k + 8], 32 * k, 1), result)
        return result

    def spread(packed):
        return jnp.concatenate(
            [packed if k == 0 else pltpu.roll(packed, 128 - 32 * k, 1) for k in range(4)], axis=0)

    gout[0, 0:8, :] = fold(kappa)
    gout[1, 0:8, :] = fold(pltpu.roll(kappa, 1, 1))

    load_zs.wait()
    for x in range(4):
        for a in range(3):
            fb[3 * x + a] = zs[pl.ds(a * 1024 + x * 8, 32, stride=32), :]
    pl.semaphore_wait(barrier, entered)
    for d in (1, 2, 3):

        @pl.when(g >= d)
        def _():
            pl.semaphore_signal(hello.at[min(d, 2) - 1], inc=1, device_id={"sub": s, "grp": slab(-d)}, device_id_type=MESH)

    halo = [
        (-1, 0, remote(ks.at[pl.ds(0, 8)], khx.at[1], hs.at[0], hr.at[0], near(-1, 0), g)),
        (1, 0, remote(ks.at[pl.ds(24, 8)], khx.at[0], hs.at[1], hr.at[1], near(1, 0), g)),
        (0, -1, remote(packy.at[0], khy.at[1], hs.at[2], hr.at[2], near(0, -1), g)),
        (0, 1, remote(packy.at[1], khy.at[0], hs.at[3], hr.at[3], near(0, 1), g)),
        (-1, -1, remote(packy.at[0], khc.at[3], hs.at[4], hr.at[4], near(-1, -1), g)),
        (1, 1, remote(packy.at[1], khc.at[0], hs.at[5], hr.at[5], near(1, 1), g)),
        (-1, 1, remote(packy.at[1], khc.at[2], hs.at[6], hr.at[6], near(-1, 1), g)),
        (1, -1, remote(packy.at[0], khc.at[1], hs.at[7], hr.at[7], near(1, -1), g)),
    ]
    for p, r, copy in halo:
        pl.when(inside(p, r))(copy.start)
    faces = [
        (1, 0, remote(planes.at[pl.ds(16 * a, 16), pl.ds(0, 8)], rx.at[pl.ds(16 * a, 16)], fs.at[a], fr.at[a], near(-1, 0), g))
        for a in range(6)
    ]
    faces.append((0, 1, remote(fb, ry, fs.at[6], fr.at[6], near(0, -1), g)))
    for p, r, copy in faces[6:] + faces[:3]:
        pl.when(inside(-p, -r))(copy.start)
    lane24 = lax.broadcasted_iota(jnp.int32, (24, 128), 1)

    def own(col):
        return jnp.concatenate(
            [zs[pl.ds(pl.multiple_of(a * 1024 + col * 32, 32), 32), :] for a in range(3)], axis=0)

    def edge(col, carry):
        first, last = carry
        u = own(col)
        for k in range(4):
            rows = u[24 * k : 24 * k + 24]
            here = lane24 == 32 * k + col
            first = jnp.where(here, pltpu.roll(rows, 32 * k + col, 1), first)
            last = jnp.where(here, pltpu.roll(rows, lax.rem(32 * k + col + 1, 128), 1), last)
        return first, last

    zero24 = jnp.zeros((24, 128), F32)
    first, last = lax.fori_loop(0, 32, edge, (zero24, zero24), unroll=UNROLL_E)
    gout[0, 8:32, :] = first
    gout[1, 8:32, :] = last

    to_low = remote(gout.at[0], gin.at[1], gs.at[0], gr.at[1], s, slab(-1))
    to_high = remote(gout.at[1], gin.at[0], gs.at[1], gr.at[0], s, slab(1))
    low_ok = g > 0
    high_ok = g < SLABS - 1
    pl.when(low_ok)(to_low.start)

    @pl.when(high_ok)
    def _():
        pl.semaphore_wait(hello.at[0], 1)
        to_high.start()

    for p, r, copy in faces[3:6]:
        pl.when(inside(-p, -r))(copy.start)
    load_c.wait()
    c_all[...] = c_in[...].astype(BF16)
    kpair = jnp.concatenate([k3[...], k3[...]], axis=1)
    c_ghost = jnp.concatenate([c_all[part * ROWS + 96 : (part + 1) * ROWS, :] for part in range(3)], axis=0)
    lane_all = lax.broadcasted_iota(jnp.int32, (ROWS, 128), 1)
    lane48 = lax.broadcasted_iota(jnp.int32, (48, 128), 1)

    def pair(step, carry):
        u = jnp.concatenate([own(2 * step), own(2 * step + 1)], axis=1)
        r = dot(c_all[...], split(u))
        rk = dot(c_ghost, split(u * kpair))
        for half in range(2):
            col = 2 * step + half
            part = r[:, 128 * half : 128 * half + 128]
            up = jnp.where(lane_all == 127, 0.0, pltpu.roll(part[ROWS : 2 * ROWS], 127, 1))
            down = jnp.where(lane_all == 0, 0.0, pltpu.roll(part[2 * ROWS :], 1, 1))
            ss[pl.ds(pl.multiple_of(col * ROWS, ROWS), ROWS), :] = part[:ROWS] + up + down
            part = rk[:, 128 * half : 128 * half + 128]
            up = jnp.where(lane48 == 127, 0.0, pltpu.roll(part[48:96], 127, 1))
            down = jnp.where(lane48 == 0, 0.0, pltpu.roll(part[96:], 1, 1))
            sgk[pl.ds(pl.multiple_of(col * 48, 48), 48), :] = part[:48] + up + down
        return carry

    lax.fori_loop(0, 16, pair, 0, unroll=UNROLL_S)

    pl.when(high_ok)(to_low.wait_recv)
    pl.when(low_ok)(to_high.wait_recv)
    lane = lax.broadcasted_iota(jnp.int32, (32, 128), 1)
    lane96 = lax.broadcasted_iota(jnp.int32, (96, 128), 1)

    h_high = spread(jnp.where(high_ok, gin[1, 8:32, :], 0.0))
    h_low = spread(jnp.where(low_ok, gin[0, 8:32, :], 0.0))
    kc_high = jnp.concatenate([spread(jnp.where(high_ok, gin[1, 0:8, :], 0.0))[:, 0:1]] * 3, axis=0)
    kc_low = jnp.concatenate([spread(jnp.where(low_ok, gin[0, 0:8, :], 0.0))[:, 0:1]] * 3, axis=0)
    edges = jnp.where(lane96 < 32, h_high, pltpu.roll(h_low, 32, 1))
    kedges = jnp.where(lane96 < 32, h_high * kc_high, pltpu.roll(h_low * kc_low, 32, 1))
    edges = jnp.where(lane96 < 64, edges, pltpu.roll(kedges, 64, 1))
    ch = dot(c_all[...], split(edges))

    for p, r, copy in halo:
        pl.when(inside(-p, -r))(copy.wait_recv)
    ke[...] = jnp.zeros_like(ke)
    for x in range(4):
        ke[1 + x, 1:9, :] = ks[8 * x : 8 * x + 8, :]
        ke[1 + x, 0:1, :] = jnp.where(inside(0, -1), khy[0, x : 1 + x, :], 0.0)
        ke[1 + x, 9:10, :] = jnp.where(inside(0, 1), khy[1, x : 1 + x, :], 0.0)
    ke[0, 1:9, :] = jnp.where(inside(-1, 0), khx[0], 0.0)
    ke[5, 1:9, :] = jnp.where(inside(1, 0), khx[1], 0.0)
    ke[0, 0:1, :] = jnp.where(inside(-1, -1), khc[0, 3:4, :], 0.0)
    ke[0, 9:10, :] = jnp.where(inside(-1, 1), khc[1, 3:4, :], 0.0)
    ke[5, 0:1, :] = jnp.where(inside(1, -1), khc[2, 0:1, :], 0.0)
    ke[5, 9:10, :] = jnp.where(inside(1, 1), khc[3, 0:1, :], 0.0)
    strips = [ke[x, 1:9, :] + 0.5 * (ke[x, 0:8, :] + ke[x, 2:10, :]) for x in range(6)]
    smooth = jnp.concatenate([strips[x + 1] + 0.5 * (strips[x] + strips[x + 2]) for x in range(4)], axis=0)
    up = jnp.where(lane == 127, 0.0, pltpu.roll(smooth, 127, 1))
    down = jnp.where(lane == 0, 0.0, pltpu.roll(smooth, 1, 1))
    kd[...] = 228.0 * ks[...] + 36.0 * smooth + 18.0 * (up + down)
    for a in range(3):
        kt[8 * a : 8 * a + 8, :] = khx[1]
        for x in range(4):
            kt[24 + 3 * x + a : 25 + 3 * x + a, :] = khy[1, x : x + 1, :]
        kt[36 + a : 37 + a, :] = khc[3, 0:1, :]
        kt[39 + a : 40 + a, :] = khc[2, 0:1, :]
    kt[42:48, :] = jnp.zeros((6, 128), F32)

    def column(tile, at):
        return jnp.concatenate([tile[:, at : at + 1]] * 3, axis=0)

    own_low = spread(gout[0, 8:32, :])
    own_high = spread(gout[1, 8:32, :])
    left = jnp.concatenate([
        h_low * (18.0 * column(smooth, 0)), h_high * (18.0 * column(smooth, 127)),
        -own_high * column(kappa, 127), -own_low * column(kappa, 0)], axis=0)
    right = jnp.concatenate([
        h_low, h_high, ch[ROWS : ROWS + 96], pltpu.roll(ch[2 * ROWS : 2 * ROWS + 96], 96, 1)], axis=0)
    outside = dot_tn(left, right)[:32, :32]

    g_high = ch[ROWS + 96 : 2 * ROWS]
    g_low = ch[2 * ROWS + 96 :]
    g_high = kt[:, 127:128] * g_high + pltpu.roll(g_high, 64, 1)
    g_low = kt[:, 0:1] * g_low + pltpu.roll(g_low, 64, 1)
    turn = jnp.where(lane48 < 32, g_high, g_low).T
    turn_high = jnp.concatenate([turn[0:32], jnp.zeros((32, 80), F32)], axis=1)
    turn_low = jnp.concatenate([turn[32:64], jnp.zeros((32, 80), F32)], axis=1)

    def ghost(step, carry):
        tiles = []
        for y in range(8):
            m = step * 8 + y
            tile = kt[pl.ds(m, 1), :] * ss[pl.ds(96 + m, 32, stride=ROWS), :] + sgk[pl.ds(m, 32, stride=48), :]
            high = jnp.where(lane == 127, pltpu.roll(turn_high, 127 - m, 1), 0.0)
            tile = tile + jnp.where(lane == 0, pltpu.roll(turn_low, lax.rem(128 - m, 128), 1), high)
            qg[m] = tile
            tiles.append(tile)
        qb[:, pl.ds(pl.multiple_of(step * 1024, 1024), 1024)] = split(jnp.concatenate(tiles, axis=1))
        return carry

    lax.fori_loop(0, 6, ghost, 0)
    corners = [
        (0, 1, remote(qg.at[pl.ds(36, 3)], qc.at[0], cs.at[0], cr.at[0], near(0, 1), g)),
        (0, -1, remote(qg.at[pl.ds(39, 3)], qc.at[1], cs.at[1], cr.at[1], near(0, -1), g)),
    ]
    for p, r, copy in corners:
        pl.when(inside(p, r))(copy.start)

    @pl.when(g < SLABS - 2)
    def _():
        pl.semaphore_wait(hello.at[1], SLABS - 2 - g)

    heard = jnp.int32(0)
    for p, r in ((1, 0), (0, 1), (0, -1)):
        heard = heard + inside(p, r).astype(jnp.int32)

        @pl.when(inside(-p, -r))
        def _():
            pl.semaphore_signal(ready, inc=1, device_id={"sub": near(-p, -r), "grp": g}, device_id_type=MESH)

    def inner(step, total):
        start_z = (step // 4) * 1024 + lax.rem(step, 4) * 8
        start_s = step * 8
        start_k = lax.rem(step, 4) * 8
        left, right = [], []
        for y in range(8):
            z = zs[pl.ds(start_z + y, 32, stride=32), :]
            v = ss[pl.ds(start_s + y, 32, stride=ROWS), :]
            left.append(z)
            right.append(kd[pl.ds(start_k + y, 1), :] * z - ks[pl.ds(start_k + y, 1), :] * v)
        left = split(jnp.concatenate(left, axis=1))
        right = split(jnp.concatenate(right, axis=1))
        return total + dot_nt(left, right)

    total = quadrants(lax.fori_loop(0, 12, inner, jnp.zeros((64, 64), F32), unroll=UNROLL_N)) + outside
    total = (total + total.T) * (1.0 / 48.0)
    nin[g, :, 0:32] = total
    sums = [remote(nin.at[g], nin.at[g], ns.at[d - 1], nr.at[d - 1], s, slab(d)) for d in (1, 2, 3)]
    for copy in sums:
        copy.start()

    flat = rx.reshape(768, 128)

    def face(a):
        return split(jnp.concatenate([flat[pl.ds(a * 256 + y, 32, stride=8), :] for y in range(8)], axis=1))

    lane32 = lax.broadcasted_iota(jnp.int32, (32, 128), 1)
    def pack(block):
        return fold(jnp.concatenate([block, jnp.zeros((32, 96), F32)], axis=1))

    def scaled(value, ok):
        return jnp.where(ok, quadrants(value) * (-1.0 / 48.0), 0.0)

    sent = []

    def give(src, slot, count, p, r, which, slabs):
        for d in slabs:
            copy = remote(src, inbox.at[g, pl.ds(slot, count)], bs.at[which, d], br.at[which, d], near(p, r), slab(d))
            pl.when(inside(p, r))(copy.start)
            sent.append((p, r, copy))

    pl.semaphore_wait(ready, heard)

    pl.when(inside(0, 1))(faces[6][2].wait_recv)
    block = scaled(dot_nt(qb[:, 24 * 128 : 36 * 128], split(jnp.concatenate([ry[t] for t in range(12)], axis=1))), inside(0, 1))
    inbox[g, 4] = pack(block)
    outbox[0] = pack(block.T)
    give(inbox.at[g, pl.ds(4, 1)], 4, 1, 0, 0, 0, (1, 2, 3))
    give(outbox.at[pl.ds(0, 1)], 3, 1, 0, 1, 1, range(4))

    for p, r, copy in corners:
        pl.when(inside(-p, -r))(copy.wait_recv)
    side = [split(jnp.concatenate([qc[e, a] for a in range(3)], axis=1)) for e in range(2)]
    value = jnp.zeros((64, 64), F32)
    value_low = jnp.zeros((64, 64), F32)
    value_high = jnp.zeros((64, 64), F32)
    for a in range(3):
        pl.when(inside(1, 0))(faces[2 * a][2].wait_recv)
        pl.when(inside(1, 0))(faces[2 * a + 1][2].wait_recv)
        f = face(a)
        value = value + dot_nt(qb[:, a * 1024 : (a + 1) * 1024], f)
        value_low = value_low + dot_nt(side[0][:, 128 * a : 128 * a + 128], f[:, 0:128])
        value_high = value_high + dot_nt(side[1][:, 128 * a : 128 * a + 128], f[:, 896:1024])
    block = scaled(value, inside(1, 0))
    block_low = scaled(value_low, inside(1, -1))
    block_high = scaled(value_high, inside(1, 1))
    inbox[g, 6] = pack(block)
    outbox[1] = pack(block_low.T)
    outbox[2] = pack(block.T)
    outbox[3] = pack(block_high.T)
    outbox[4] = pack(block_low)
    outbox[5] = pack(block_high)
    give(outbox.at[pl.ds(1, 3)], 0, 3, 1, 0, 2, (2, 3, 1, 0))
    give(inbox.at[g, pl.ds(6, 1)], 6, 1, 0, 0, 5, (2, 3, 1))
    give(outbox.at[pl.ds(4, 1)], 7, 1, 0, -1, 3, (2, 3, 1, 0))
    give(outbox.at[pl.ds(5, 1)], 5, 1, 0, 1, 4, (2, 3, 1, 0))

    for copy in sums:
        copy.wait_recv()
    row32 = lax.broadcasted_iota(jnp.int32, (32, 128), 0)
    m = nin[0] + nin[1] + nin[2] + nin[3]
    m = jnp.where(lane32 < 32, m, jnp.where(lane32 == row32 + 32, 1.0, 0.0))
    lower = jnp.zeros((32, 128), F32)
    for k in range(32):
        pivot = m[k : k + 1, k : k + 1]
        r = lax.rsqrt(pivot)
        r = r * (1.5 - 0.5 * pivot * r * r)
        col = m[:, k : k + 1] * r
        line = m[k : k + 1, :] * r
        lower = jnp.where(jnp.logical_and(lane32 == k, row32 >= k), col, lower)
        m = jnp.where(row32 > k, m - col * line, jnp.where(row32 == k, line, m))
    factor[...] = lower[:, 0:32] * (1.0 / np.sqrt(49152.0))
    inverse = m[:, 32:64]

    for p, r, copy in sent:
        pl.when(inside(-p, -r))(copy.wait_recv)
    packed = [jnp.where(inside(*ALL_NEAR[b]), inbox[0, b] + inbox[1, b] + inbox[2, b] + inbox[3, b], 0.0) for b in range(8)]
    halves = []
    for part in range(2):
        rows = []
        for k in range(4):
            result = jnp.zeros((8, 128), F32)
            for at in range(4):
                shift = (32 * (at - k)) % 128
                moved = packed[4 * part + at]
                moved = moved if shift == 0 else pltpu.roll(moved, shift, 1)
                result = jnp.where(lane8 // 32 == at, moved, result)
            rows.append(result)
        halves.append(jnp.concatenate(rows, axis=0))
    every = jnp.concatenate(halves, axis=1)
    solved = lax.dot_general(inverse, every, (((1,), (0,)), ((), ())), precision=lax.Precision.HIGHEST,
                             preferred_element_type=F32)
    for b in range(8):
        panel[b] = solved[:, 32 * b : 32 * b + 32]

    pl.when(low_ok)(to_low.wait_send)
    pl.when(high_ok)(to_high.wait_send)
    for copy in sums:
        copy.wait_send()
    for p, r, copy in halo + sent:
        pl.when(inside(p, r))(copy.wait_send)
    for p, r, copy in faces:
        pl.when(inside(-p, -r))(copy.wait_send)
    for p, r, copy in corners:
        pl.when(inside(p, r))(copy.wait_send)


def shards(stencil, basis, material, kappa_table):
    hbm = pl.BlockSpec(memory_space=pltpu.HBM)
    vmem = pl.BlockSpec(memory_space=pltpu.VMEM)
    dma = pltpu.SemaphoreType.DMA
    operands = (basis.reshape(3072, 128), basis.reshape(96, 32, 128), material.reshape(32, 128), kappa_table, stencil)
    factor, panel = pl.pallas_call(
        kernel,
        out_shape=(jax.ShapeDtypeStruct((32, 32), F32), jax.ShapeDtypeStruct((8, 32, 32), F32)),
        in_specs=[hbm] * 5,
        out_specs=(vmem, vmem),
        scratch_shapes=[
            pltpu.VMEM((3072, 128), F32),
            pltpu.VMEM((32, 128), jnp.int32),
            pltpu.VMEM((3 * ROWS, 192), BF16),
            pltpu.VMEM((12, 32, 128), F32),
            pltpu.VMEM((96, 8, 128), F32),
            pltpu.VMEM((12, 32, 128), F32),
            pltpu.VMEM((32, 128), F32),
            pltpu.VMEM((2, 8, 128), F32),
            pltpu.VMEM((2, 32, 128), F32),
            pltpu.VMEM((2, 32, 128), F32),
            pltpu.VMEM((2, 8, 128), F32),
            pltpu.VMEM((2, 8, 128), F32),
            pltpu.VMEM((4, 8, 128), F32),
            pltpu.VMEM((6, 16, 128), F32),
            pltpu.VMEM((32, 128), F32),
            pltpu.VMEM((48, 128), F32),
            pltpu.VMEM((96, 128), F32),
            pltpu.VMEM((32 * ROWS, 128), F32),
            pltpu.VMEM((32 * 48, 128), F32),
            pltpu.VMEM((64, 6 * 1024), BF16),
            pltpu.VMEM((48, 32, 128), F32),
            pltpu.VMEM((2, 3, 32, 128), F32),
            pltpu.VMEM((4, 32, 128), F32),
            pltpu.VMEM((4, 8, 8, 128), F32),
            pltpu.VMEM((6, 8, 128), F32),
            pltpu.SMEM((8,), F32),
            pltpu.VMEM((3 * ROWS, 192), F32),
            pltpu.SemaphoreType.REGULAR((2,)), pltpu.SemaphoreType.REGULAR,
            dma((4,)), dma((2,)), dma((2,)), dma((8,)), dma((8,)), dma((7,)), dma((7,)), dma((2,)), dma((2,)),
            dma((3,)), dma((3,)), dma((6, 4)), dma((6, 4)),
        ],
        compiler_params=pltpu.CompilerParams(
            collective_id=0, has_side_effects=True, vmem_limit_bytes=40 * 2**20),
        name="coarse_blocks",
    )(*(pltpu.with_memory_space_constraint(value, pltpu.HBM) for value in operands))
    return factor[None], panel[None]


def solution(mesh):
    placed = (P(), P("sub", None, None, None, None, "grp"), P("sub", None, None, "grp"), P())
    call = jax.shard_map(
        shards,
        mesh=mesh,
        in_specs=placed,
        out_specs=(P("sub", None, None), P("sub", None, None, None)),
        check_vma=False,
    )
    matrix = stencil_matrix()

    def run(basis, material, kappa_table):
        return call(jnp.asarray(matrix, F32), basis, material, kappa_table)

    return run
```

```python
import functools

import jax
import jax.numpy as jnp
import numpy as np
from jax import lax
from jax.experimental import pallas as pl
from jax.experimental.pallas import tpu as pltpu
from jax.sharding import PartitionSpec as P

YDOMS = 4
XDOMS = 16
SLABS = 4
MESH = pl.DeviceIdType.MESH
F32 = jnp.float32
BF16 = jnp.bfloat16
GHOSTS = 42
ROWS = 144
ALL_NEAR = [(p, r) for p in (-1, 0, 1) for r in (-1, 0, 1) if (p, r) != (0, 0)]
UNROLL_E = 32
UNROLL_S = 2
UNROLL_N = 2


def out_cells():
    cells = [(a, x, y) for a in range(3) for x in range(4) for y in range(8)]
    cells += [(a, 4, y) for a in range(3) for y in range(8)]
    cells += [(a, x, 8) for x in range(4) for a in range(3)]
    cells += [(a, 4, 8) for a in range(3)]
    cells += [(a, 4, -1) for a in range(3)]
    return cells


def stencil_matrix():
    whole = np.zeros((3, ROWS, 96), np.float64)
    for part, step_z in enumerate((0, 1, -1)):
        for row, (a, x, y) in enumerate(out_cells()):
            for p in (-1, 0, 1):
                for r in (-1, 0, 1):
                    o = (p, r, step_z)
                    q = sum(v * v for v in o)
                    if q == 0 or not (0 <= x + p < 4 and 0 <= y + r < 8):
                        continue
                    for b in range(3):
                        g = (1.0 if a == b else 0.0) + 0.5 / q * o[a] * o[b]
                        whole[part, row, b * 32 + (x + p) * 8 + y + r] += 24.0 * 0.5 ** (q - 1) * g
    whole = np.round(whole).reshape(3 * ROWS, 96)
    return np.concatenate([whole, whole], axis=1)


def split(value):
    high = value.astype(BF16)
    low = (value - high.astype(F32)).astype(BF16)
    return jnp.concatenate([high, low], axis=0)


def dot(a, b):
    return lax.dot_general(a, b, (((1,), (0,)), ((), ())), preferred_element_type=F32)


def dot_nt(a, b):
    return lax.dot_general(a, b, (((1,), (1,)), ((), ())), preferred_element_type=F32)


def dot_tn(a, b):
    return lax.dot_general(a, b, (((0,), (0,)), ((), ())), precision=lax.Precision.HIGHEST, preferred_element_type=F32)


def quadrants(r):
    top = r[:32] + r[32:]
    return top[:, :32] + top[:, 32:]


def kernel(basis, planes, material, table, stencil, factor, panel,
           zs, mat, c_all, fb, rx, ry, ks, packy, gin, gout, khx, khy, khc, ke, kd, kt, k3,
           ss, sgk, qb, qg, qc, nin, inbox, outbox, tab, c_in,
           hello, ready, lsem, gs, gr, hs, hr, fs, fr, cs, cr, ns, nr, bs, br):
    s = lax.axis_index("sub")
    g = lax.axis_index("grp")
    i = s // YDOMS
    j = lax.rem(s, YDOMS)

    def near(p, r):
        return lax.rem(i + p + XDOMS, XDOMS) * YDOMS + lax.rem(j + r + YDOMS, YDOMS)

    def inside(p, r):
        ok = i >= 0
        if p:
            ok = jnp.logical_and(ok, i < XDOMS - 1 if p > 0 else i > 0)
        if r:
            ok = jnp.logical_and(ok, j < YDOMS - 1 if r > 0 else j > 0)
        return ok

    def slab(d):
        return lax.rem(g + d + SLABS, SLABS)

    def remote(src, dst, send, recv, sub, grp):
        return pltpu.make_async_remote_copy(
            src_ref=src, dst_ref=dst, send_sem=send, recv_sem=recv,
            device_id={"sub": sub, "grp": grp}, device_id_type=MESH)

    barrier = pltpu.get_barrier_semaphore()
    entered = g
    for p, r in ALL_NEAR:
        entered = entered + inside(p, r).astype(jnp.int32)

        @pl.when(inside(p, r))
        def _():
            pl.semaphore_signal(barrier, inc=1, device_id={"sub": near(p, r), "grp": g}, device_id_type=MESH)

    for d in (1, 2, 3):

        @pl.when(g + d < SLABS)
        def _():
            pl.semaphore_signal(barrier, inc=1, device_id={"sub": s, "grp": slab(d)}, device_id_type=MESH)

    load_mat = pltpu.make_async_copy(material, mat, lsem.at[0])
    load_zs = pltpu.make_async_copy(basis, zs, lsem.at[1])
    load_c = pltpu.make_async_copy(stencil, c_in, lsem.at[2])
    load_tab = pltpu.make_async_copy(table, tab, lsem.at[3])
    load_mat.start()
    load_tab.start()
    load_zs.start()
    load_c.start()

    load_mat.wait()
    load_tab.wait()
    ids = mat[...]
    kappa = jnp.zeros((32, 128), F32)
    for which in range(8):
        kappa = kappa + jnp.where(ids == which, tab[which], 0.0)
    ks[...] = kappa
    for e, y in ((0, 0), (1, 7)):
        for x in range(4):
            packy[e, x : x + 1, :] = ks[8 * x + y : 8 * x + y + 1, :]
    for a in range(3):
        k3[32 * a : 32 * a + 32, :] = kappa
    lane8 = lax.broadcasted_iota(jnp.int32, (8, 128), 1)

    def fold(wide):
        result = wide[0:8]
        for k in range(1, 4):
            result = jnp.where(lane8 // 32 == k, pltpu.roll(wide[8 * k : 8 * k + 8], 32 * k, 1), result)
        return result

    def spread(packed):
        return jnp.concatenate(
            [packed if k == 0 else pltpu.roll(packed, 128 - 32 * k, 1) for k in range(4)], axis=0)

    gout[0, 0:8, :] = fold(kappa)
    gout[1, 0:8, :] = fold(pltpu.roll(kappa, 1, 1))

    load_zs.wait()
    for x in range(4):
        for a in range(3):
            fb[3 * x + a] = zs[pl.ds(a * 1024 + x * 8, 32, stride=32), :]
    pl.semaphore_wait(barrier, entered)
    for d in (1, 2, 3):

        @pl.when(g >= d)
        def _():
            pl.semaphore_signal(hello.at[min(d, 2) - 1], inc=1, device_id={"sub": s, "grp": slab(-d)}, device_id_type=MESH)

    halo = [
        (-1, 0, remote(ks.at[pl.ds(0, 8)], khx.at[1], hs.at[0], hr.at[0], near(-1, 0), g)),
        (1, 0, remote(ks.at[pl.ds(24, 8)], khx.at[0], hs.at[1], hr.at[1], near(1, 0), g)),
        (0, -1, remote(packy.at[0], khy.at[1], hs.at[2], hr.at[2], near(0, -1), g)),
        (0, 1, remote(packy.at[1], khy.at[0], hs.at[3], hr.at[3], near(0, 1), g)),
        (-1, -1, remote(packy.at[0], khc.at[3], hs.at[4], hr.at[4], near(-1, -1), g)),
        (1, 1, remote(packy.at[1], khc.at[0], hs.at[5], hr.at[5], near(1, 1), g)),
        (-1, 1, remote(packy.at[1], khc.at[2], hs.at[6], hr.at[6], near(-1, 1), g)),
        (1, -1, remote(packy.at[0], khc.at[1], hs.at[7], hr.at[7], near(1, -1), g)),
    ]
    for p, r, copy in halo:
        pl.when(inside(p, r))(copy.start)
    faces = [
        (1, 0, remote(planes.at[pl.ds(16 * a, 16), pl.ds(0, 8)], rx.at[pl.ds(16 * a, 16)], fs.at[a], fr.at[a], near(-1, 0), g))
        for a in range(6)
    ]
    faces.append((0, 1, remote(fb, ry, fs.at[6], fr.at[6], near(0, -1), g)))
    for p, r, copy in faces[6:] + faces[:3]:
        pl.when(inside(-p, -r))(copy.start)
    lane24 = lax.broadcasted_iota(jnp.int32, (24, 128), 1)

    def own(col):
        return jnp.concatenate(
            [zs[pl.ds(pl.multiple_of(a * 1024 + col * 32, 32), 32), :] for a in range(3)], axis=0)

    def edge(col, carry):
        first, last = carry
        u = own(col)
        for k in range(4):
            rows = u[24 * k : 24 * k + 24]
            here = lane24 == 32 * k + col
            first = jnp.where(here, pltpu.roll(rows, 32 * k + col, 1), first)
            last = jnp.where(here, pltpu.roll(rows, lax.rem(32 * k + col + 1, 128), 1), last)
        return first, last

    zero24 = jnp.zeros((24, 128), F32)
    first, last = lax.fori_loop(0, 32, edge, (zero24, zero24), unroll=UNROLL_E)
    gout[0, 8:32, :] = first
    gout[1, 8:32, :] = last

    to_low = remote(gout.at[0], gin.at[1], gs.at[0], gr.at[1], s, slab(-1))
    to_high = remote(gout.at[1], gin.at[0], gs.at[1], gr.at[0], s, slab(1))
    low_ok = g > 0
    high_ok = g < SLABS - 1
    pl.when(low_ok)(to_low.start)

    @pl.when(high_ok)
    def _():
        pl.semaphore_wait(hello.at[0], 1)
        to_high.start()

    for p, r, copy in faces[3:6]:
        pl.when(inside(-p, -r))(copy.start)
    load_c.wait()
    c_all[...] = c_in[...].astype(BF16)
    kpair = jnp.concatenate([k3[...], k3[...]], axis=1)
    c_ghost = jnp.concatenate([c_all[part * ROWS + 96 : (part + 1) * ROWS, :] for part in range(3)], axis=0)
    lane_all = lax.broadcasted_iota(jnp.int32, (ROWS, 128), 1)
    lane48 = lax.broadcasted_iota(jnp.int32, (48, 128), 1)

    def pair(step, carry):
        u = jnp.concatenate([own(2 * step), own(2 * step + 1)], axis=1)
        r = dot(c_all[...], split(u))
        rk = dot(c_ghost, split(u * kpair))
        for half in range(2):
            col = 2 * step + half
            part = r[:, 128 * half : 128 * half + 128]
            up = jnp.where(lane_all == 127, 0.0, pltpu.roll(part[ROWS : 2 * ROWS], 127, 1))
            down = jnp.where(lane_all == 0, 0.0, pltpu.roll(part[2 * ROWS :], 1, 1))
            ss[pl.ds(pl.multiple_of(col * ROWS, ROWS), ROWS), :] = part[:ROWS] + up + down
            part = rk[:, 128 * half : 128 * half + 128]
            up = jnp.where(lane48 == 127, 0.0, pltpu.roll(part[48:96], 127, 1))
            down = jnp.where(lane48 == 0, 0.0, pltpu.roll(part[96:], 1, 1))
            sgk[pl.ds(pl.multiple_of(col * 48, 48), 48), :] = part[:48] + up + down
        return carry

    lax.fori_loop(0, 16, pair, 0, unroll=UNROLL_S)

    pl.when(high_ok)(to_low.wait_recv)
    pl.when(low_ok)(to_high.wait_recv)
    lane = lax.broadcasted_iota(jnp.int32, (32, 128), 1)
    lane96 = lax.broadcasted_iota(jnp.int32, (96, 128), 1)

    h_high = spread(jnp.where(high_ok, gin[1, 8:32, :], 0.0))
    h_low = spread(jnp.where(low_ok, gin[0, 8:32, :], 0.0))
    kc_high = jnp.concatenate([spread(jnp.where(high_ok, gin[1, 0:8, :], 0.0))[:, 0:1]] * 3, axis=0)
    kc_low = jnp.concatenate([spread(jnp.where(low_ok, gin[0, 0:8, :], 0.0))[:, 0:1]] * 3, axis=0)
    edges = jnp.where(lane96 < 32, h_high, pltpu.roll(h_low, 32, 1))
    kedges = jnp.where(lane96 < 32, h_high * kc_high, pltpu.roll(h_low * kc_low, 32, 1))
    edges = jnp.where(lane96 < 64, edges, pltpu.roll(kedges, 64, 1))
    ch = dot(c_all[...], split(edges))

    for p, r, copy in halo:
        pl.when(inside(-p, -r))(copy.wait_recv)
    ke[...] = jnp.zeros_like(ke)
    for x in range(4):
        ke[1 + x, 1:9, :] = ks[8 * x : 8 * x + 8, :]
        ke[1 + x, 0:1, :] = jnp.where(inside(0, -1), khy[0, x : 1 + x, :], 0.0)
        ke[1 + x, 9:10, :] = jnp.where(inside(0, 1), khy[1, x : 1 + x, :], 0.0)
    ke[0, 1:9, :] = jnp.where(inside(-1, 0), khx[0], 0.0)
    ke[5, 1:9, :] = jnp.where(inside(1, 0), khx[1], 0.0)
    ke[0, 0:1, :] = jnp.where(inside(-1, -1), khc[0, 3:4, :], 0.0)
    ke[0, 9:10, :] = jnp.where(inside(-1, 1), khc[1, 3:4, :], 0.0)
    ke[5, 0:1, :] = jnp.where(inside(1, -1), khc[2, 0:1, :], 0.0)
    ke[5, 9:10, :] = jnp.where(inside(1, 1), khc[3, 0:1, :], 0.0)
    strips = [ke[x, 1:9, :] + 0.5 * (ke[x, 0:8, :] + ke[x, 2:10, :]) for x in range(6)]
    smooth = jnp.concatenate([strips[x + 1] + 0.5 * (strips[x] + strips[x + 2]) for x in range(4)], axis=0)
    up = jnp.where(lane == 127, 0.0, pltpu.roll(smooth, 127, 1))
    down = jnp.where(lane == 0, 0.0, pltpu.roll(smooth, 1, 1))
    kd[...] = 228.0 * ks[...] + 36.0 * smooth + 18.0 * (up + down)
    for a in range(3):
        kt[8 * a : 8 * a + 8, :] = khx[1]
        for x in range(4):
            kt[24 + 3 * x + a : 25 + 3 * x + a, :] = khy[1, x : x + 1, :]
        kt[36 + a : 37 + a, :] = khc[3, 0:1, :]
        kt[39 + a : 40 + a, :] = khc[2, 0:1, :]
    kt[42:48, :] = jnp.zeros((6, 128), F32)

    def column(tile, at):
        return jnp.concatenate([tile[:, at : at + 1]] * 3, axis=0)

    own_low = spread(gout[0, 8:32, :])
    own_high = spread(gout[1, 8:32, :])
    left = jnp.concatenate([
        h_low * (18.0 * column(smooth, 0)), h_high * (18.0 * column(smooth, 127)),
        -own_high * column(kappa, 127), -own_low * column(kappa, 0)], axis=0)
    right = jnp.concatenate([
        h_low, h_high, ch[ROWS : ROWS + 96], pltpu.roll(ch[2 * ROWS : 2 * ROWS + 96], 96, 1)], axis=0)
    outside = dot_tn(left, right)[:32, :32]

    g_high = ch[ROWS + 96 : 2 * ROWS]
    g_low = ch[2 * ROWS + 96 :]
    g_high = kt[:, 127:128] * g_high + pltpu.roll(g_high, 64, 1)
    g_low = kt[:, 0:1] * g_low + pltpu.roll(g_low, 64, 1)
    turn = jnp.where(lane48 < 32, g_high, g_low).T
    turn_high = jnp.concatenate([turn[0:32], jnp.zeros((32, 80), F32)], axis=1)
    turn_low = jnp.concatenate([turn[32:64], jnp.zeros((32, 80), F32)], axis=1)

    def ghost(step, carry):
        tiles = []
        for y in range(8):
            m = step * 8 + y
            tile = kt[pl.ds(m, 1), :] * ss[pl.ds(96 + m, 32, stride=ROWS), :] + sgk[pl.ds(m, 32, stride=48), :]
            high = jnp.where(lane == 127, pltpu.roll(turn_high, 127 - m, 1), 0.0)
            tile = tile + jnp.where(lane == 0, pltpu.roll(turn_low, lax.rem(128 - m, 128), 1), high)
            qg[m] = tile
            tiles.append(tile)
        qb[:, pl.ds(pl.multiple_of(step * 1024, 1024), 1024)] = split(jnp.concatenate(tiles, axis=1))
        return carry

    lax.fori_loop(0, 6, ghost, 0)
    corners = [
        (0, 1, remote(qg.at[pl.ds(36, 3)], qc.at[0], cs.at[0], cr.at[0], near(0, 1), g)),
        (0, -1, remote(qg.at[pl.ds(39, 3)], qc.at[1], cs.at[1], cr.at[1], near(0, -1), g)),
    ]
    for p, r, copy in corners:
        pl.when(inside(p, r))(copy.start)

    @pl.when(g < SLABS - 2)
    def _():
        pl.semaphore_wait(hello.at[1], SLABS - 2 - g)

    heard = jnp.int32(0)
    for p, r in ((1, 0), (0, 1), (0, -1)):
        heard = heard + inside(p, r).astype(jnp.int32)

        @pl.when(inside(-p, -r))
        def _():
            pl.semaphore_signal(ready, inc=1, device_id={"sub": near(-p, -r), "grp": g}, device_id_type=MESH)

    def inner(step, total):
        start_z = (step // 4) * 1024 + lax.rem(step, 4) * 8
        start_s = step * 8
        start_k = lax.rem(step, 4) * 8
        left, right = [], []
        for y in range(8):
            z = zs[pl.ds(start_z + y, 32, stride=32), :]
            v = ss[pl.ds(start_s + y, 32, stride=ROWS), :]
            left.append(z)
            right.append(kd[pl.ds(start_k + y, 1), :] * z - ks[pl.ds(start_k + y, 1), :] * v)
        left = split(jnp.concatenate(left, axis=1))
        right = split(jnp.concatenate(right, axis=1))
        return total + dot_nt(left, right)

    total = quadrants(lax.fori_loop(0, 12, inner, jnp.zeros((64, 64), F32), unroll=UNROLL_N)) + outside
    total = (total + total.T) * (1.0 / 48.0)
    nin[g, :, 0:32] = total
    sums = [remote(nin.at[g], nin.at[g], ns.at[d - 1], nr.at[d - 1], s, slab(d)) for d in (1, 2, 3)]
    for copy in sums:
        copy.start()

    flat = rx.reshape(768, 128)

    def face(a):
        return split(jnp.concatenate([flat[pl.ds(a * 256 + y, 32, stride=8), :] for y in range(8)], axis=1))

    lane32 = lax.broadcasted_iota(jnp.int32, (32, 128), 1)
    def pack(block):
        return fold(jnp.concatenate([block, jnp.zeros((32, 96), F32)], axis=1))

    def scaled(value, ok):
        return jnp.where(ok, quadrants(value) * (-1.0 / 48.0), 0.0)

    sent = []

    def give(src, slot, count, p, r, which, slabs):
        for d in slabs:
            copy = remote(src, inbox.at[g, pl.ds(slot, count)], bs.at[which, d], br.at[which, d], near(p, r), slab(d))
            pl.when(inside(p, r))(copy.start)
            sent.append((p, r, copy))

    pl.semaphore_wait(ready, heard)

    pl.when(inside(0, 1))(faces[6][2].wait_recv)
    block = scaled(dot_nt(qb[:, 24 * 128 : 36 * 128], split(jnp.concatenate([ry[t] for t in range(12)], axis=1))), inside(0, 1))
    inbox[g, 4] = pack(block)
    outbox[0] = pack(block.T)
    give(inbox.at[g, pl.ds(4, 1)], 4, 1, 0, 0, 0, (1, 2, 3))
    give(outbox.at[pl.ds(0, 1)], 3, 1, 0, 1, 1, range(4))

    for p, r, copy in corners:
        pl.when(inside(-p, -r))(copy.wait_recv)
    side = [split(jnp.concatenate([qc[e, a] for a in range(3)], axis=1)) for e in range(2)]
    value = jnp.zeros((64, 64), F32)
    value_low = jnp.zeros((64, 64), F32)
    value_high = jnp.zeros((64, 64), F32)
    for a in range(3):
        pl.when(inside(1, 0))(faces[2 * a][2].wait_recv)
        pl.when(inside(1, 0))(faces[2 * a + 1][2].wait_recv)
        f = face(a)
        value = value + dot_nt(qb[:, a * 1024 : (a + 1) * 1024], f)
        value_low = value_low + dot_nt(side[0][:, 128 * a : 128 * a + 128], f[:, 0:128])
        value_high = value_high + dot_nt(side[1][:, 128 * a : 128 * a + 128], f[:, 896:1024])
    block = scaled(value, inside(1, 0))
    block_low = scaled(value_low, inside(1, -1))
    block_high = scaled(value_high, inside(1, 1))
    inbox[g, 6] = pack(block)
    outbox[1] = pack(block_low.T)
    outbox[2] = pack(block.T)
    outbox[3] = pack(block_high.T)
    outbox[4] = pack(block_low)
    outbox[5] = pack(block_high)
    give(outbox.at[pl.ds(1, 3)], 0, 3, 1, 0, 2, (2, 3, 1, 0))
    give(inbox.at[g, pl.ds(6, 1)], 6, 1, 0, 0, 5, (2, 3, 1))
    give(outbox.at[pl.ds(4, 1)], 7, 1, 0, -1, 3, (2, 3, 1, 0))
    give(outbox.at[pl.ds(5, 1)], 5, 1, 0, 1, 4, (2, 3, 1, 0))

    for copy in sums:
        copy.wait_recv()
    row32 = lax.broadcasted_iota(jnp.int32, (32, 128), 0)
    m = nin[0] + nin[1] + nin[2] + nin[3]
    m = jnp.where(lane32 < 32, m, jnp.where(lane32 == row32 + 32, 1.0, 0.0))
    lower = jnp.zeros((32, 128), F32)
    for k in range(32):
        pivot = m[k : k + 1, k : k + 1]
        r = lax.rsqrt(pivot)
        r = r * (1.5 - 0.5 * pivot * r * r)
        col = m[:, k : k + 1] * r
        line = m[k : k + 1, :] * r
        lower = jnp.where(jnp.logical_and(lane32 == k, row32 >= k), col, lower)
        m = jnp.where(row32 > k, m - col * line, jnp.where(row32 == k, line, m))
    factor[...] = lower[:, 0:32] * (1.0 / np.sqrt(49152.0))
    inverse = m[:, 32:64]

    for p, r, copy in sent:
        pl.when(inside(-p, -r))(copy.wait_recv)
    packed = [jnp.where(inside(*ALL_NEAR[b]), inbox[0, b] + inbox[1, b] + inbox[2, b] + inbox[3, b], 0.0) for b in range(8)]
    halves = []
    for part in range(2):
        rows = []
        for k in range(4):
            result = jnp.zeros((8, 128), F32)
            for at in range(4):
                shift = (32 * (at - k)) % 128
                moved = packed[4 * part + at]
                moved = moved if shift == 0 else pltpu.roll(moved, shift, 1)
                result = jnp.where(lane8 // 32 == at, moved, result)
            rows.append(result)
        halves.append(jnp.concatenate(rows, axis=0))
    every = jnp.concatenate(halves, axis=1)
    solved = lax.dot_general(inverse, every, (((1,), (0,)), ((), ())), precision=lax.Precision.HIGHEST,
                             preferred_element_type=F32)
    for b in range(8):
        panel[b] = solved[:, 32 * b : 32 * b + 32]

    pl.when(low_ok)(to_low.wait_send)
    pl.when(high_ok)(to_high.wait_send)
    for copy in sums:
        copy.wait_send()
    for p, r, copy in halo + sent:
        pl.when(inside(p, r))(copy.wait_send)
    for p, r, copy in faces:
        pl.when(inside(-p, -r))(copy.wait_send)
    for p, r, copy in corners:
        pl.when(inside(p, r))(copy.wait_send)


def shards(stencil, basis, material, kappa_table):
    hbm = pl.BlockSpec(memory_space=pltpu.HBM)
    vmem = pl.BlockSpec(memory_space=pltpu.VMEM)
    dma = pltpu.SemaphoreType.DMA
    operands = (basis.reshape(3072, 128), basis.reshape(96, 32, 128), material.reshape(32, 128), kappa_table, stencil)
    factor, panel = pl.pallas_call(
        kernel,
        out_shape=(jax.ShapeDtypeStruct((32, 32), F32), jax.ShapeDtypeStruct((8, 32, 32), F32)),
        in_specs=[hbm] * 5,
        out_specs=(vmem, vmem),
        scratch_shapes=[
            pltpu.VMEM((3072, 128), F32),
            pltpu.VMEM((32, 128), jnp.int32),
            pltpu.VMEM((3 * ROWS, 192), BF16),
            pltpu.VMEM((12, 32, 128), F32),
            pltpu.VMEM((96, 8, 128), F32),
            pltpu.VMEM((12, 32, 128), F32),
            pltpu.VMEM((32, 128), F32),
            pltpu.VMEM((2, 8, 128), F32),
            pltpu.VMEM((2, 32, 128), F32),
            pltpu.VMEM((2, 32, 128), F32),
            pltpu.VMEM((2, 8, 128), F32),
            pltpu.VMEM((2, 8, 128), F32),
            pltpu.VMEM((4, 8, 128), F32),
            pltpu.VMEM((6, 16, 128), F32),
            pltpu.VMEM((32, 128), F32),
            pltpu.VMEM((48, 128), F32),
            pltpu.VMEM((96, 128), F32),
            pltpu.VMEM((32 * ROWS, 128), F32),
            pltpu.VMEM((32 * 48, 128), F32),
            pltpu.VMEM((64, 6 * 1024), BF16),
            pltpu.VMEM((48, 32, 128), F32),
            pltpu.VMEM((2, 3, 32, 128), F32),
            pltpu.VMEM((4, 32, 128), F32),
            pltpu.VMEM((4, 8, 8, 128), F32),
            pltpu.VMEM((6, 8, 128), F32),
            pltpu.SMEM((8,), F32),
            pltpu.VMEM((3 * ROWS, 192), F32),
            pltpu.SemaphoreType.REGULAR((2,)), pltpu.SemaphoreType.REGULAR,
            dma((4,)), dma((2,)), dma((2,)), dma((8,)), dma((8,)), dma((7,)), dma((7,)), dma((2,)), dma((2,)),
            dma((3,)), dma((3,)), dma((6, 4)), dma((6, 4)),
        ],
        compiler_params=pltpu.CompilerParams(
            collective_id=0, has_side_effects=True, vmem_limit_bytes=40 * 2**20),
        name="coarse_blocks",
    )(*(pltpu.with_memory_space_constraint(value, pltpu.HBM) for value in operands))
    return factor[None], panel[None]


def solution(mesh):
    placed = (P(), P("sub", None, None, None, None, "grp"), P("sub", None, None, "grp"), P())
    call = jax.shard_map(
        shards,
        mesh=mesh,
        in_specs=placed,
        out_specs=(P("sub", None, None), P("sub", None, None, None)),
        check_vma=False,
    )
    matrix = stencil_matrix()

    def run(basis, material, kappa_table):
        return call(jnp.asarray(matrix, F32), basis, material, kappa_table)

    return run
```
